32 devices in a mesh: dp: 2 (over core), row: 4 (over y, x), col: 4 (over z).
Axes of the slice: x: 2, y: 2, z: 4, core: 2. Of those that a mesh axis runs over, the one named last changes fastest.
Arguments:
- tokens: bfloat16 [4096, 2048], P(('dp', 'col'), 'row'), may hold values from -6 to 6
- segment_ids: int32 [2, 2048], P('dp'), may hold values from 0 to 2, never falling along the last dimension, each value on 1 to 1536 neighbouring positions
- ln1_gain: bfloat16 [2048], P('row'), may hold values from 0.25 to 1.75
- ln1_bias: bfloat16 [2048], P('row'), may hold values from -3 to 3
- w_query: bfloat16 [2048, 2048], P('row', 'col'), may hold values from -0.125 to 0.125
- b_query: bfloat16 [2048], P('col'), may hold values from -3 to 3
- w_keyval: bfloat16 [2048, 256], P('row'), may hold values from -0.125 to 0.125
- b_value: bfloat16 [128], replicated, may hold values from -1.1953125 to 1.1953125
- w_out: bfloat16 [2048, 2048], P('col', 'row'), may hold values from -0.5 to 0.5
- b_out: bfloat16 [2048], P('row'), may hold values from -2 to 2
- ln2_gain: bfloat16 [2048], P('row'), may hold values from 0.25 to 1.75
- ln2_bias: bfloat16 [2048], P('row'), may hold values from -3 to 3
- w_up: bfloat16 [2048, 8192], P('row', 'col'), may hold values from -0.16572815 to 0.16572815
- b_up: bfloat16 [8192], P('col'), may hold values from -3 to 3
- w_down: bfloat16 [8192, 2048], P('col', 'row'), may hold values from -0.0625 to 0.0625
- b_down: bfloat16 [2048], P('row'), may hold values from -2 to 2
- d_output: bfloat16 [4096, 2048], P(('dp', 'col'), 'row'), may hold values from -6 to 6
Outputs:
- output: bfloat16 [4096, 2048], P(('dp', 'col'), 'row')
- grad_tokens: float32 [4096, 2048], P(('dp', 'col'), 'row')
- grad_ln1_gain: float32 [2048], P('row')
- grad_ln1_bias: float32 [2048], P('row')
- grad_w_query: float32 [2048, 2048], P('row', 'col')
- grad_b_query: float32 [2048], P('col')
- grad_w_keyval: float32 [2048, 256], P('row')
- grad_b_value: float32 [128], replicated
- grad_w_out: float32 [2048, 2048], P('col', 'row')
- grad_b_out: float32 [2048], P('row')
- grad_ln2_gain: float32 [2048], P('row')
- grad_ln2_bias: float32 [2048], P('row')
- grad_w_up: float32 [2048, 8192], P('row', 'col')
- grad_b_up: float32 [8192], P('col')
- grad_w_down: float32 [8192, 2048], P('col', 'row')
- grad_b_down: float32 [2048], P('row')
The draws below stay inside these ranges and needn't reach their ends.
Inputs may be any that keep to these rules, and one draw needn't show every extreme that they name: `segment_ids`: in each sequence the segment ids never fall; each document holds 1 to 1536 tokens, and one holds exactly 1536.
All inputs are finite; a program needn't handle non-finite values.
Results may differ from the reference program's by a relative error of at most 0.014.
Values may be sent and summed in bfloat16 or wider, within the bound.
No kernel may reach another device: no remote copies, remote signals or barrier semaphores. Data moves between devices by JAX's collectives and lax.ppermute only.
A program may use at most 320 MiB of HBM per device.

```python
import math
import jax
import jax.numpy as jnp
import numpy as np
from jax import lax

D = 2048
HEADS = 16
HEAD = 128
FF = 8192
TOK_DP = 2048
SEQS = 2
TOKENS = 4096
DOC_COUNT = 3
DOC_MOST = 1536


def draw_w_up(key, part):
    key = jax.random.fold_in(key, 11)
    entry_key, column_key = jax.random.split(key)
    entries = jnp.clip(jax.random.normal(entry_key, (D, FF), jnp.float32), -6.0, 6.0)
    columns = jnp.clip(0.5 * jax.random.normal(column_key, (1, FF), jnp.float32), -1.5, 1.5)
    return ((entries + columns) * D ** (-0.5)).astype(jnp.bfloat16)


def shard_levels(rng, dims, cuts, smallest, top_value):
    def one(dim, blocks):
        steps = jax.random.uniform(jax.random.fold_in(jax.random.fold_in(rng, 6), dim), (blocks,), jnp.float32, smallest / len(cuts), top_value / len(cuts))
        return jnp.repeat(jnp.exp(steps), dims[dim] // blocks).reshape((-1,) + (1,) * (len(dims) - dim - 1))

    level = one(*cuts[0])
    for cut in cuts[1:]:
        level = level * one(*cut)
    return level


def length_profile(number_of, total, bound, skew):
    weights = [(1 << 20) // math.isqrt(rank ** skew) + 1 for rank in range(2, number_of + 1)]
    spare, counts = total - bound - (number_of - 1), [1] * (number_of - 1)
    while spare > 0:
        candidates = [i for i in range(number_of - 1) if counts[i] < bound]
        pool, budget = sum([weights[i] for i in candidates]), spare
        for i in candidates:
            addition = min(bound - counts[i], max(1, budget * weights[i] // pool), spare)
            counts[i] = counts[i] + addition
            spare = spare - addition
    return np.array([bound] + counts)


def ragged(rng, amount, total, bound, slope):
    if amount == 2:
        one = jax.random.randint(rng, (), max(1, total - bound), min(bound, total - 1) + 1)
        return jnp.stack([one, total - one])
    tallies = jnp.asarray(length_profile(amount, total, bound, slope), jnp.int32)
    couples = (amount - 1) // 2
    donor, sink = tallies[1:1 + 2 * couples:2], tallies[2:2 + 2 * couples:2]
    room = jnp.minimum(donor - 1, bound - sink)
    passed = jax.random.randint(jax.random.fold_in(rng, 1), (couples,), 0, 1 << 20) % (room + 1)
    tallies = tallies.at[1:1 + 2 * couples:2].set(donor - passed).at[2:2 + 2 * couples:2].set(sink + passed)
    return tallies[jax.random.permutation(jax.random.fold_in(rng, 2), amount)]


def noise(stream_key, shape, scale, most, cuts=(), held_as=jnp.bfloat16):
    level = shard_levels(stream_key, shape, cuts, -0.22, 0.18) if cuts else 1.0
    values = jax.random.normal(stream_key, shape, jnp.float32) * scale * level
    return jnp.minimum(jnp.maximum(values, -most), most).astype(held_as)


def setup_inputs(seed: int = 0) -> dict:
    streams_of = jax.random.split(jax.random.key(seed), 18)
    return {
        "tokens": noise(streams_of[0], (TOKENS, D), 1.0, 6.0, ((0, 8), (1, 4))),
        "segment_ids": jax.vmap(lambda own: jnp.searchsorted(jnp.cumsum(ragged(own, DOC_COUNT, TOK_DP, DOC_MOST, 1)), jnp.arange(TOK_DP), side="right"))(jax.random.split(streams_of[1], SEQS)).reshape((SEQS, TOK_DP)).astype(jnp.int32),
        "ln1_gain": jnp.clip(1.0 + 0.15 * jax.random.normal(streams_of[2], (D,), jnp.float32), 0.25, 1.75).astype(jnp.bfloat16),
        "ln1_bias": noise(streams_of[3], (D,), 0.3, 3.0, ((0, 4),)),
        "w_query": noise(streams_of[4], (D, D), D ** -0.5, 0.125, ((0, 4), (1, 4))),
        "b_query": noise(streams_of[5], (D,), 0.5, 3.0, ((0, 4),)),
        "w_keyval": noise(streams_of[6], (D, 2 * HEAD), D ** -0.5, 0.125, ((0, 4),)),
        "b_value": noise(streams_of[7], (HEAD,), 0.2, 1.1953125),
        "w_out": noise(streams_of[8], (D, D), (D // 16) ** -0.5, 0.5, ((0, 4), (1, 4))),
        "b_out": noise(streams_of[9], (D,), 0.3, 2.0, ((0, 4),)),
        "ln2_gain": jnp.clip(1.0 + 0.15 * jax.random.normal(streams_of[10], (D,), jnp.float32), 0.25, 1.75).astype(jnp.bfloat16),
        "ln2_bias": noise(streams_of[11], (D,), 0.3, 3.0, ((0, 4),)),
        "w_up": draw_w_up(jax.random.fold_in(streams_of[17], 71), 0),
        "b_up": noise(streams_of[13], (FF,), 0.5, 3.0, ((0, 4),)),
        "w_down": noise(streams_of[14], (FF, D), FF ** -0.5, 0.0625, ((0, 4), (1, 4))),
        "b_down": noise(streams_of[15], (D,), 0.3, 2.0, ((0, 4),)),
        "d_output": noise(streams_of[16], (TOKENS, D), 1.0, 6.0, ((0, 8), (1, 4))),
    }


@jax.custom_vjp
def low(v):
    return lax.optimization_barrier(v.astype(jnp.bfloat16)).astype(jnp.float32)

@jax.custom_vjp
def low_back(v):
    return v

def low_keep(v):
    return (low(v), None)

def low_pass(kept, grad):
    return (grad,)

def back_keep(v):
    return (v, None)

def back_low(kept, grad):
    return (low(grad),)
low.defvjp(low_keep, low_pass)
low_back.defvjp(back_keep, back_low)
epsilon = 1e-05
negative = -1e+30

def matmul(left, right):
    return jnp.dot(left, right, precision=lax.Precision.HIGHEST, preferred_element_type=jnp.float32)

def layer_norm(values, gain, offset):
    average = lax.optimization_barrier(jnp.mean(values, axis=-1, keepdims=True))
    spread = lax.optimization_barrier(jnp.mean(values * values, axis=-1, keepdims=True)) - average * average
    return (values - average) * lax.rsqrt(spread + epsilon) * gain + offset

def attention(queries, keys, values, segments):
    length = queries.shape[0]
    block_rows = min(512, length)
    block_count = length // block_rows
    heads_view = queries.reshape(block_count, block_rows, HEADS, HEAD)
    starts = jnp.arange(block_count, dtype=jnp.int32) * block_rows
    key_pos = jnp.arange(length, dtype=jnp.int32)
    scaling = HEAD ** (-0.5)

    def one_block(block_item):
        query_block, block_start = block_item
        scores = jnp.einsum('thd,kd->thk', query_block, keys, precision=lax.Precision.HIGHEST) * scaling
        query_pos = block_start + jnp.arange(block_rows, dtype=jnp.int32)
        query_seg = lax.dynamic_slice_in_dim(segments, block_start, block_rows)
        allowed = (query_seg[:, None, None] == segments[None, None, :]) & (key_pos[None, None, :] <= query_pos[:, None, None])
        scores = low_back(jnp.where(allowed, scores, negative))
        shifted = scores - lax.optimization_barrier(jnp.max(scores, axis=-1, keepdims=True))
        expo = jnp.exp(shifted)
        probs = low(expo / lax.optimization_barrier(jnp.sum(expo, axis=-1, keepdims=True)))
        return jnp.einsum('thk,kd->thd', probs, values, precision=lax.Precision.HIGHEST)
    blocks = lax.map(jax.checkpoint(one_block), (heads_view, starts))
    return blocks.reshape(length, HEADS * HEAD)

def layer(tokens, segments, params):
    gain_one, bias_one, w_query, b_query, w_keyval, b_value, w_out, b_out, gain_two, bias_two, w_up, b_up, w_down, b_down = params
    normed_one = low(layer_norm(tokens, gain_one, bias_one))
    queries = low_back(low(matmul(normed_one, w_query) + b_query))
    keyval = matmul(normed_one, w_keyval)
    keys = low_back(low(keyval[:, :HEAD]))
    values = low_back(low(keyval[:, HEAD:] + b_value))
    attended = low_back(low(attention(queries, keys, values, segments)))
    hidden_one = tokens + low_back(matmul(attended, w_out) + b_out)
    normed_two = low(layer_norm(hidden_one, gain_two, bias_two))
    upper = low_back(matmul(normed_two, w_up) + b_up)
    activated = low(jax.nn.gelu(upper, approximate=True))
    return hidden_one + low_back(matmul(activated, w_down) + b_down)

def reference(tokens, segment_ids, ln1_gain, ln1_bias, w_query, b_query, w_keyval, b_value, w_out, b_out, ln2_gain, ln2_bias, w_up, b_up, w_down, b_down, d_output):
    params = tuple((param_array.astype(jnp.float32) for param_array in (ln1_gain, ln1_bias, w_query, b_query, w_keyval, b_value, w_out, b_out, ln2_gain, ln2_bias, w_up, b_up, w_down, b_down)))
    inputs = tokens.astype(jnp.float32).reshape(SEQS, TOK_DP, D)
    cotangents = d_output.astype(jnp.float32).reshape(SEQS, TOK_DP, D)

    def one_sequence(running, sequence_item):
        seq_tokens, seq_segments, seq_grad = sequence_item
        result, pullback = jax.vjp(lambda inner_tokens, inner_params: layer(inner_tokens, seq_segments, inner_params), seq_tokens, params)
        grad_input, grad_params = pullback(seq_grad)
        running = jax.tree.map(lambda first_sum, second_sum: first_sum + second_sum, running, grad_params)
        return (running, (result, grad_input))
    zeros = jax.tree.map(jnp.zeros_like, params)
    totals, (results, grad_inputs) = lax.scan(one_sequence, zeros, (inputs, segment_ids, cotangents))
    return (results.reshape(TOKENS, D).astype(jnp.bfloat16), grad_inputs.reshape(TOKENS, D), totals[0], totals[1], totals[2], totals[3], totals[4], totals[5], totals[6], totals[7], totals[8], totals[9], totals[10], totals[11], totals[12], totals[13])
```

```python
import functools
import math

import jax
import jax.numpy as jnp
from jax import lax
from jax.experimental import pallas as pl
from jax.experimental.pallas import tpu as pltpu
from jax.sharding import Mesh
from jax.sharding import PartitionSpec as P

epsilon = 1e-05
negative = -1e30
log2e = math.log2(math.e)
f32 = jnp.float32
bf16 = jnp.bfloat16


def dot_nn(a, b):
    return lax.dot_general(a, b, (((1,), (0,)), ((), ())), preferred_element_type=f32)


def dot_nt(a, b):
    return lax.dot_general(a, b, (((1,), (1,)), ((), ())), preferred_element_type=f32)


def dot_tn(a, b):
    return lax.dot_general(a, b, (((0,), (0,)), ((), ())), preferred_element_type=f32)


def swap(a, axis):
    return lax.ppermute(a, axis, [(0, 1), (1, 0)])


def cross(a):
    return lax.ppermute(a, ("rx", "cl"), [(0, 3), (1, 2), (2, 1), (3, 0)])


def fetch(a, axis, step):
    n = lax.axis_size(axis)
    return lax.ppermute(a, axis, [(s, (s - step) % n) for s in range(n)])


def after(a, b):
    return lax.optimization_barrier((a, b))[0]


def block_gather(a):
    return jnp.concatenate([a, swap(a, "rx"), swap(a, "cl"), cross(a)], axis=0)


def block_scatter(p):
    t = p.shape[0] // 4
    low = p.astype(bf16)
    got_x = swap(low[t : 2 * t], "rx")
    got_z = swap(low[2 * t : 3 * t], "cl")
    got_d = cross(low[3 * t :])
    return p[:t] + got_x.astype(f32) + got_z.astype(f32) + got_d.astype(f32)


def end_swap(a):
    return lax.ppermute(a, ("ch", "cl"), [(1, 2), (2, 1)])


def line_gather(a):
    far = swap(a, "ch")
    near = swap(a, "cl")
    mid = end_swap(a)
    end = lax.ppermute(far, ("ch", "cl"), [(1, 0), (2, 3)])
    return jnp.concatenate([a, near, far, mid + end], axis=0)


def line_scatter(p):
    t = p.shape[0] // 4
    low = p.astype(bf16)
    end = lax.ppermute(low[3 * t :], ("ch", "cl"), [(0, 1), (3, 2)])
    near = swap(low[t : 2 * t], "cl")
    far = swap((p[2 * t : 3 * t] + end.astype(f32)).astype(bf16), "ch")
    mid = end_swap(low[3 * t :])
    return p[:t] + near.astype(f32) + far.astype(f32) + mid.astype(f32)


def gather_axis(a, axis):
    n = lax.axis_size(axis)
    if n == 2:
        b = swap(a, axis)
        first = lax.axis_index(axis) == 0
        return jnp.stack([jnp.where(first, a, b), jnp.where(first, b, a)])
    return lax.all_gather(a, axis, axis=0, tiled=False)


def scatter_axis(a, axis):
    n = lax.axis_size(axis)
    me = lax.axis_index(axis)
    total = lax.dynamic_index_in_dim(a, me, 0, keepdims=False)
    for step in range(1, n):
        part = lax.dynamic_index_in_dim(a, (me - step) % n, 0, keepdims=False)
        total = total + fetch(part.astype(bf16), axis, step).astype(f32)
    return total


def sum_small(v):
    for axis in ("dp", "rx", "cl", "ch", "ry"):
        if lax.axis_size(axis) == 2:
            v = v + swap(v, axis)
        else:
            v = lax.psum(v, axis)
    return v


def half_of(w, axis):
    n = w.shape[axis] // 2
    return lax.dynamic_slice_in_dim(w, lax.axis_index("dp") * n, n, axis)


def scatter_rows(g, feat):
    every = ("ry", "rx", "dp")
    n = 1
    for axis in every:
        n *= lax.axis_size(axis)
    g = g.astype(bf16)
    if feat == 1:
        g = g.reshape(g.shape[0], n, g.shape[1] // n).transpose(1, 0, 2)
    else:
        g = g.reshape(n, g.shape[0] // n, g.shape[1])
    part = lax.psum_scatter(g, every, scatter_dimension=0, tiled=False)
    pair = gather_axis(part, "dp")
    return jnp.concatenate([pair[0], pair[1]], axis=feat).astype(f32)


class Place:
    def __init__(self):
        self.dp = lax.axis_index("dp")
        self.ry = lax.axis_index("ry")
        self.rx = lax.axis_index("rx")
        self.ch = lax.axis_index("ch")
        self.cl = lax.axis_index("cl")
        self.rows_y = lax.axis_size("ry")
        self.rows = 2 * self.rows_y

    def row_of(self, k):
        return ((self.ry + k // 2) % self.rows_y) * 2 + (self.rx ^ (k % 2))

    def slot_of(self, r):
        return ((r // 2 - self.ry) % self.rows_y) * 2 + (self.rx ^ (r % 2))

    def to_relative(self, a):
        w = a.shape[1] // self.rows
        return jnp.concatenate(
            [lax.dynamic_slice_in_dim(a, self.row_of(k) * w, w, 1) for k in range(self.rows)], axis=1
        )

    def to_absolute(self, a):
        w = a.shape[1] // self.rows
        return jnp.concatenate(
            [lax.dynamic_slice_in_dim(a, self.slot_of(r) * w, w, 1) for r in range(self.rows)], axis=1
        )

    def hidden_part(self, w, half, quarter, axis):
        q = w.shape[axis] // 4
        return lax.dynamic_slice_in_dim(w, (half * 2 + quarter) * q, q, axis)

    def gather_weight(self, w, hidden):
        feat = 1 - hidden
        mine = self.hidden_part(w, self.rx, self.dp, hidden)
        theirs = self.hidden_part(w, 1 - self.rx, self.dp, hidden)
        block = jnp.concatenate([mine, swap(theirs, "rx")], axis=feat)
        other = swap(block, "ch")
        parts = []
        for b in (block, other):
            b = jnp.concatenate([b] + [fetch(b, "ry", j) for j in range(1, self.rows_y)], axis=feat)
            parts += [b, swap(b, "dp")]
        return jnp.concatenate(parts, axis=hidden)

    def gather_hidden(self, b):
        mine = jnp.concatenate(
            [self.hidden_part(b, self.rx, self.dp, 0), self.hidden_part(b, self.rx, 1 - self.dp, 0)]
        )
        return jnp.concatenate([mine, swap(mine, "ch")])

    def scatter_weight(self, g, hidden):
        feat = 1 - hidden
        q = g.shape[hidden] // 4
        cut = lambda a, lo, n, axis: lax.slice_in_dim(a, lo, lo + n, axis=axis)
        got = swap(
            jnp.concatenate([cut(g, q, q, hidden), cut(g, 3 * q, q, hidden)], axis=hidden).astype(bf16), "dp"
        )
        own = jnp.concatenate([cut(g, 0, q, hidden), cut(g, 2 * q, q, hidden)], axis=hidden)
        total = own + got.astype(f32)
        span = g.shape[feat] // self.rows_y
        part = cut(total, 0, span, feat)
        for j in range(1, self.rows_y):
            sent = cut(total, j * span, span, feat).astype(bf16)
            n = self.rows_y
            part = part + lax.ppermute(sent, "ry", [(s, (s + j) % n) for s in range(n)]).astype(f32)
        part = cut(part, 0, q, hidden) + swap(cut(part, q, q, hidden).astype(bf16), "ch").astype(f32)
        part = part.astype(bf16)
        width = span // 2
        pair = jnp.concatenate([cut(part, 0, width, feat), swap(cut(part, width, width, feat), "rx")], axis=hidden)
        far = swap(pair, "dp")
        pieces = [[cut(pair, 0, q, hidden), cut(far, 0, q, hidden)], [cut(pair, q, q, hidden), cut(far, q, q, hidden)]]
        out = []
        for i in range(2):
            for d in range(2):
                near = jnp.where(self.dp == d, pieces[i][0], pieces[i][1])
                away = jnp.where(self.dp == d, pieces[1 - i][0], pieces[1 - i][1])
                out.append(jnp.where(self.rx == 0, near, away))
        return jnp.concatenate(out, axis=hidden).astype(f32)

    def place_hidden(self, v, blocks):
        q = v.shape[0] // 4
        whole = jnp.zeros((blocks * 4 * q,), f32)
        for a in range(2):
            for d in range(2):
                c = (self.ch ^ a) * 2 + self.cl
                start = c * 4 * q + (self.rx * 2 + (self.dp ^ d)) * q
                k = 2 * a + d
                whole = lax.dynamic_update_slice_in_dim(whole, v[k * q : (k + 1) * q], start, 0)
        return whole


def stack_heads(a, heads):
    w = a.shape[1] // heads
    return jnp.concatenate([a[:, h * w : (h + 1) * w] for h in range(heads)], axis=0)


def attend_forward(
    bounds, q_ref, k_ref, v_ref, low_ref, pos_ref, o_ref, lse_ref, *, heads, span, scale
):
    chunk = pl.program_id(0)
    rows = stack_heads(q_ref[...], heads)
    n, width = rows.shape
    low = jnp.concatenate([low_ref[0]] * heads, axis=1)
    pos = jnp.concatenate([pos_ref[0]] * heads, axis=1)

    def step(kb, state):
        top, total, acc = state
        start = pl.multiple_of(kb * span, span)
        keys = k_ref[pl.ds(start, span), :]
        values = v_ref[pl.ds(start, span), :]
        s = dot_nt(keys, rows) * scale
        at = start + lax.broadcasted_iota(jnp.int32, (span, n), 0)
        s = jnp.where((at >= low) & (at <= pos), s, negative)
        new = jnp.maximum(top, jnp.max(s, axis=0, keepdims=True))
        p = jnp.exp2(s - new)
        fade = jnp.exp2(top - new)
        total = total * fade + jnp.sum(p, axis=0, keepdims=True)
        acc = acc * fade + dot_tn(values, p.astype(bf16))
        return new, total, acc

    start_state = (
        jnp.full((1, n), negative, f32),
        jnp.zeros((1, n), f32),
        jnp.zeros((width, n), f32),
    )
    top, total, acc = lax.fori_loop(bounds[chunk, 0], bounds[chunk, 1], step, start_state)
    out = (acc / total).T.astype(bf16)
    t = n // heads
    for h in range(heads):
        o_ref[:, h * width : (h + 1) * width] = out[h * t : (h + 1) * t]
    lse_ref[0] = top + jnp.log2(total)


def attend_backward(
    bounds, q_ref, o_ref, g_ref, lse_ref, k_ref, v_ref, low_ref, pos_ref, dq_ref, dkv_ref, *, heads, span, scale, plain
):
    chunk = pl.program_id(0)

    @pl.when(chunk == 0)
    def _():
        dkv_ref[...] = jnp.zeros_like(dkv_ref)

    rows = stack_heads(q_ref[...], heads)
    outs = stack_heads(o_ref[...], heads)
    grads = stack_heads(g_ref[...], heads)
    n, width = rows.shape
    low = jnp.concatenate([low_ref[0]] * heads, axis=1)
    pos = jnp.concatenate([pos_ref[0]] * heads, axis=1)
    lse = lse_ref[0]
    delta = jnp.sum((outs.astype(f32) * grads.astype(f32)).T, axis=0, keepdims=True)

    def step(kb, acc):
        start = pl.multiple_of(kb * span, span)
        keys = k_ref[pl.ds(start, span), :]
        values = v_ref[pl.ds(start, span), :]
        s = dot_nt(keys, rows) * scale
        at = start + lax.broadcasted_iota(jnp.int32, (span, n), 0)
        p = jnp.where((at >= low) & (at <= pos), jnp.exp2(s - lse), 0.0)
        dp = dot_nt(values, grads)
        ds = (p * (dp - delta)).astype(bf16)
        acc = acc + dot_tn(keys, ds)
        dkv_ref[pl.ds(start, span), :width] += dot_nn(ds, rows) * plain
        dkv_ref[pl.ds(start, span), width:] += dot_nn(p.astype(bf16), grads)
        return acc

    acc = lax.fori_loop(bounds[chunk, 0], bounds[chunk, 1], step, jnp.zeros((width, n), f32))
    out = (acc * plain).T.astype(bf16)
    t = n // heads
    for h in range(heads):
        dq_ref[:, h * width : (h + 1) * width] = out[h * t : (h + 1) * t]


class Attention:
    def __init__(self, tokens, chunks, hidden, length, head):
        self.t, self.chunks, self.hidden, self.length, self.head = tokens, chunks, hidden, length, head
        self.heads = hidden // head
        self.span = min(512, length)
        self.plain = head ** (-0.5)
        self.scale = self.plain * log2e
        self.params = pltpu.CompilerParams(
            dimension_semantics=("arbitrary",), vmem_limit_bytes=48 * 1024 * 1024
        )
        self.rows_spec = pl.BlockSpec((tokens, hidden), lambda i, b: (i, 0))
        self.kv_spec = pl.BlockSpec((length, head), lambda i, b: (0, 0))
        self.vec_spec = pl.BlockSpec((1, 1, tokens), lambda i, b: (i, 0, 0))
        self.lse_spec = pl.BlockSpec((1, 1, tokens * self.heads), lambda i, b: (i, 0, 0))
        self.cells = tokens * chunks * self.heads * length

    def forward(self, bounds, q, k, v, low, pos):
        body = functools.partial(attend_forward, heads=self.heads, span=self.span, scale=self.scale)
        return pl.pallas_call(
            body,
            grid_spec=pltpu.PrefetchScalarGridSpec(
                num_scalar_prefetch=1,
                grid=(self.chunks,),
                in_specs=[self.rows_spec, self.kv_spec, self.kv_spec, self.vec_spec, self.vec_spec],
                out_specs=[self.rows_spec, self.lse_spec],
            ),
            out_shape=[
                jax.ShapeDtypeStruct(q.shape, bf16),
                jax.ShapeDtypeStruct((self.chunks, 1, self.t * self.heads), f32),
            ],
            compiler_params=self.params,
            cost_estimate=pl.CostEstimate(
                flops=4 * self.cells * self.head, bytes_accessed=4 << 20, transcendentals=self.cells
            ),
        )(bounds, q, k, v, low, pos)

    def backward(self, bounds, q, o, g, lse, k, v, low, pos):
        body = functools.partial(
            attend_backward, heads=self.heads, span=self.span, scale=self.scale, plain=self.plain
        )
        return pl.pallas_call(
            body,
            grid_spec=pltpu.PrefetchScalarGridSpec(
                num_scalar_prefetch=1,
                grid=(self.chunks,),
                in_specs=[self.rows_spec] * 3
                + [self.lse_spec, self.kv_spec, self.kv_spec, self.vec_spec, self.vec_spec],
                out_specs=[
                    self.rows_spec,
                    pl.BlockSpec((self.length, 2 * self.head), lambda i, b: (0, 0)),
                ],
            ),
            out_shape=[
                jax.ShapeDtypeStruct(q.shape, bf16),
                jax.ShapeDtypeStruct((self.length, 2 * self.head), f32),
            ],
            compiler_params=self.params,
            cost_estimate=pl.CostEstimate(
                flops=10 * self.cells * self.head, bytes_accessed=8 << 20, transcendentals=self.cells
            ),
        )(bounds, q, o, g, lse, k, v, low, pos)


def norm_parts(v):
    mean = jnp.mean(v, axis=1, keepdims=True)
    spread = jnp.mean(v * v, axis=1, keepdims=True) - mean * mean
    inv_std = lax.rsqrt(spread + epsilon)
    return (v - mean) * inv_std, inv_std


def norm_back(e, centred, inv_std, gain):
    c = e * gain
    m1 = jnp.mean(c, axis=1, keepdims=True)
    m2 = jnp.mean(c * centred, axis=1, keepdims=True)
    return (c - m1 - centred * m2) * inv_std


gelu_a = math.sqrt(2.0 / math.pi)
gelu_b = 0.044715


def gelu(u):
    return 0.5 * u * (1.0 + jnp.tanh(gelu_a * (u + gelu_b * u * u * u)))


def gelu_slope(u):
    th = jnp.tanh(gelu_a * (u + gelu_b * u * u * u))
    return 0.5 * (1.0 + th) + 0.5 * u * (1.0 - th * th) * gelu_a * (1.0 + 3.0 * gelu_b * u * u)


def per_device(
    tokens,
    segment_ids,
    ln1_gain,
    ln1_bias,
    w_query,
    b_query,
    w_keyval,
    b_value,
    w_out,
    b_out,
    ln2_gain,
    ln2_bias,
    w_up,
    b_up,
    w_down,
    b_down,
    d_output,
):
    at = Place()
    rows = at.rows
    blocks = 2 * lax.axis_size("ch")
    col_tokens, row_width = tokens.shape
    t = col_tokens // rows
    width = row_width * rows
    head = b_value.shape[0]
    length = segment_ids.shape[1]
    row_axes = ("ry", "rx")
    row = at.ry * 2 + at.rx
    col = at.ch * 2 + at.cl

    vectors = jnp.stack([ln1_gain, ln1_bias, ln2_gain, ln2_bias, b_out, b_down])
    vectors = gather_axis(gather_axis(vectors, "rx"), "ry")
    vectors = vectors.transpose(2, 0, 1, 3).reshape(6, 1, width).astype(f32)
    gain_one, bias_one, gain_two, bias_two, out_bias, down_bias = vectors

    own = lax.all_to_all(tokens, row_axes, 0, 1, tiled=True).astype(f32)
    own_grad = lax.all_to_all(d_output, row_axes, 0, 1, tiled=True)

    kv_weight = gather_axis(gather_axis(w_keyval, "rx"), "ry").reshape(width, 2 * head)
    query_weight = at.gather_weight(w_query, 1)
    out_weight = at.gather_weight(after(w_out, query_weight), 0)
    every = ("ry", "rx", "dp")
    up_weight = lax.all_gather(half_of(w_up, 0), every, axis=0, tiled=True)
    down_weight = lax.all_gather(half_of(w_down, 1), every, axis=1, tiled=True)
    query_bias = at.gather_hidden(b_query).astype(f32)
    up_bias = b_up.astype(f32)

    segments = segment_ids[0]
    base = jnp.stack(
        [
            ((at.ch * 2 + (at.cl ^ (k // 2))) * col_tokens + (at.ry * 2 + (at.rx ^ (k % 2))) * t)
            for k in range(4)
        ]
    ).astype(jnp.int32)
    pos = base[:, None] + jnp.arange(t, dtype=jnp.int32)[None, :]
    seg_rows = jnp.stack([lax.dynamic_slice_in_dim(segments, base[k], t, 0) for k in range(4)])
    low = jnp.sum((segments[None, None, :] < seg_rows[:, :, None]).astype(jnp.int32), axis=2)
    attention = Attention(t, 4, query_weight.shape[1], length, head)
    span = attention.span
    bounds = jnp.stack([low[:, 0] // span, (base + t - 1) // span + 1], axis=1)
    low, pos = low[:, None, :], pos[:, None, :]

    centred_one, inv_one = norm_parts(own)
    normed_one = (centred_one * gain_one + bias_one).astype(bf16)
    kv_own = dot_nn(normed_one, kv_weight)
    kv_own = jnp.concatenate([kv_own[:, :head], kv_own[:, head:] + b_value.astype(f32)], axis=1).astype(bf16)
    kv = kv_own
    for axis in ("ch", "cl", "ry", "rx"):
        kv = gather_axis(kv, axis)
    kv = kv.transpose(3, 2, 1, 0, 4, 5).reshape(length, 2 * head)
    keys, values = kv[:, :head], kv[:, head:]
    block_one = at.to_relative(block_gather(normed_one))
    queries = (dot_nn(block_one, query_weight) + query_bias).astype(bf16)
    attended, lse = attention.forward(bounds, queries, keys, values, low, pos)

    hidden_one = own + out_bias + block_scatter(at.to_absolute(dot_nn(attended, out_weight)))
    centred_two, inv_two = norm_parts(hidden_one)
    normed_two = (centred_two * gain_two + bias_two).astype(bf16)
    block_two = line_gather(normed_two)

    block_grad = line_gather(own_grad)
    upper = dot_nn(block_two, up_weight) + up_bias
    activated = gelu(upper).astype(bf16)
    grad_upper = (dot_nt(block_grad, down_weight) * gelu_slope(upper)).astype(bf16)
    grad_two = line_scatter(dot_nt(grad_upper, up_weight))
    grad_w_down = scatter_rows(dot_tn(activated, block_grad), 1)
    grad_w_up = scatter_rows(dot_tn(block_two, grad_upper), 0)
    final = hidden_one + down_bias + line_scatter(dot_nn(after(activated, grad_two), down_weight))
    output = lax.all_to_all(final.astype(bf16), row_axes, 1, 0, tiled=True)

    grad_hidden = own_grad.astype(f32) + norm_back(grad_two, centred_two, inv_two, gain_two)
    grad_branch = grad_hidden.astype(bf16)
    block_branch = at.to_relative(block_gather(grad_branch))
    grad_w_out = at.scatter_weight(dot_tn(attended, block_branch), 0)
    grad_att = dot_nt(block_branch, out_weight).astype(bf16)
    grad_query, grad_kv = attention.backward(
        bounds, queries, attended, grad_att, lse, keys, values, low, pos
    )
    grad_kv = grad_kv.reshape(blocks // 2, 2, rows // 2, 2, t, 2 * head)
    grad_kv = grad_kv.transpose(3, 1, 2, 0, 4, 5)
    for axis in ("rx", "cl", "ry", "ch"):
        grad_kv = scatter_axis(grad_kv, axis)
    kv_grad_own = grad_kv.astype(bf16)
    grad_one = block_scatter(at.to_absolute(dot_nt(grad_query, query_weight)))
    grad_one = grad_one + dot_nt(kv_grad_own, kv_weight)
    grad_w_query = at.scatter_weight(dot_tn(block_one, grad_query), 1)
    grad_own = grad_hidden + norm_back(grad_one, centred_one, inv_one, gain_one)
    grad_tokens = lax.all_to_all(grad_own.astype(bf16), row_axes, 1, 0, tiled=True).astype(f32)

    kv_part = dot_tn(normed_one, kv_grad_own).reshape(rows // 2, 2, row_width, 2 * head).transpose(1, 0, 2, 3)
    for axis in ("rx", "ry"):
        kv_part = scatter_axis(kv_part, axis)
    for axis in ("cl", "ch", "dp"):
        if lax.axis_size(axis) == 2:
            kv_part = kv_part.astype(bf16)
            kv_part = kv_part.astype(f32) + swap(kv_part, axis).astype(f32)
        else:
            kv_part = lax.psum(kv_part, axis)
    grad_w_keyval = kv_part

    sums = lambda a: jnp.sum(a.astype(f32), axis=0)
    early = jnp.concatenate(
        [
            lax.dynamic_update_slice_in_dim(
                jnp.zeros((b_up.shape[0] * blocks,), f32), sums(grad_upper), col * b_up.shape[0], 0
            ),
            sums(own_grad),
            sums(grad_branch),
            sums(grad_two * centred_two),
            sums(grad_two),
        ]
    )
    late = jnp.concatenate(
        [
            at.place_hidden(sums(grad_query), blocks),
            sums(grad_one * centred_one),
            sums(grad_one),
            sums(kv_grad_own[:, head:]),
        ]
    )
    early, late = sum_small(early), sum_small(late)
    hid = b_up.shape[0]
    of_col = lambda v, n: lax.dynamic_slice_in_dim(v, col * n, n, 0)
    of_row = lambda v, at_: lax.dynamic_slice_in_dim(v, at_ + row * row_width, row_width, 0)
    top = hid * blocks
    grad_b_up = of_col(early, hid)
    grad_b_down = of_row(early, top)
    grad_b_out = of_row(early, top + width)
    grad_ln2_gain = of_row(early, top + 2 * width)
    grad_ln2_bias = of_row(early, top + 3 * width)
    hid = b_query.shape[0]
    top = hid * blocks
    grad_b_query = of_col(late, hid)
    grad_ln1_gain = of_row(late, top)
    grad_ln1_bias = of_row(late, top + width)
    grad_b_value = late[top + 2 * width :]
    return (
        output,
        grad_tokens,
        grad_ln1_gain,
        grad_ln1_bias,
        grad_w_query,
        grad_b_query,
        grad_w_keyval,
        grad_b_value,
        grad_w_out,
        grad_b_out,
        grad_ln2_gain,
        grad_ln2_bias,
        grad_w_up,
        grad_b_up,
        grad_w_down,
        grad_b_down,
    )


def solution(mesh):
    dp, rows, cols = (mesh.shape[name] for name in ("dp", "row", "col"))
    fine = Mesh(
        mesh.devices.reshape(dp, rows // 2, 2, cols // 2, 2), ("dp", "ry", "rx", "ch", "cl")
    )
    row, col = ("ry", "rx"), ("ch", "cl")
    tok = P(("dp", "ch", "cl"), row)
    in_specs = (
        tok,
        P("dp", None),
        P(row),
        P(row),
        P(row, col),
        P(col),
        P(row, None),
        P(),
        P(col, row),
        P(row),
        P(row),
        P(row),
        P(row, col),
        P(col),
        P(col, row),
        P(row),
        tok,
    )
    out_specs = (
        tok,
        tok,
        P(row),
        P(row),
        P(row, col),
        P(col),
        P(row, None),
        P(),
        P(col, row),
        P(row),
        P(row),
        P(row),
        P(row, col),
        P(col),
        P(col, row),
        P(row),
    )
    return jax.shard_map(
        per_device, mesh=fine, in_specs=in_specs, out_specs=out_specs, check_vma=False
    )
```

```python
import functools
import math

import jax
import jax.numpy as jnp
from jax import lax
from jax.experimental import pallas as pl
from jax.experimental.pallas import tpu as pltpu
from jax.sharding import Mesh
from jax.sharding import PartitionSpec as P

epsilon = 1e-05
negative = -1e30
log2e = math.log2(math.e)
f32 = jnp.float32
bf16 = jnp.bfloat16


def dot_nn(a, b):
    return lax.dot_general(a, b, (((1,), (0,)), ((), ())), preferred_element_type=f32)


def dot_nt(a, b):
    return lax.dot_general(a, b, (((1,), (1,)), ((), ())), preferred_element_type=f32)


def dot_tn(a, b):
    return lax.dot_general(a, b, (((0,), (0,)), ((), ())), preferred_element_type=f32)


def swap(a, axis):
    return lax.ppermute(a, axis, [(0, 1), (1, 0)])


def fetch(a, axis, step):
    n = lax.axis_size(axis)
    return lax.ppermute(a, axis, [(s, (s - step) % n) for s in range(n)])


def tie(*arrays):
    return jax.tree.unflatten(
        jax.tree.structure(arrays), lax.optimization_barrier(tuple(jax.tree.leaves(arrays)))
    )


def add(u, v):
    return (u.astype(f32) + v.astype(f32)).astype(bf16)


def end_swap(a):
    return lax.ppermute(a, ("ch", "cl"), [(1, 2), (2, 1)])


def line_first(a):
    return swap(a, "ch"), swap(a, "cl"), end_swap(a)


def line_second(a, far, near, mid):
    end = lax.ppermute(far, ("ch", "cl"), [(1, 0), (2, 3)])
    return jnp.concatenate([a, near, far, mid + end], axis=0)


def line_scatter_first(p):
    t = p.shape[0] // 4
    end = lax.ppermute(p[3 * t :], ("ch", "cl"), [(0, 1), (3, 2)])
    return end, swap(p[t : 2 * t], "cl"), end_swap(p[3 * t :])


def line_scatter_second(p, end):
    t = p.shape[0] // 4
    return swap(add(p[2 * t : 3 * t], end), "ch")


def line_total(p, near, mid, far):
    t = p.shape[0] // 4
    return p[:t].astype(f32) + near.astype(f32) + far.astype(f32) + mid.astype(f32)


def gather_axis(a, axis):
    n = lax.axis_size(axis)
    if n == 2:
        b = swap(a, axis)
        first = lax.axis_index(axis) == 0
        return jnp.stack([jnp.where(first, a, b), jnp.where(first, b, a)])
    return lax.all_gather(a, axis, axis=0, tiled=False)


def row_send(a, k, rows):
    n, j, i = rows // 2, k // 2, k % 2
    pairs = [(y * 2 + x, (y + j) % n * 2 + (x ^ i)) for y in range(n) for x in range(2)]
    return lax.ppermute(a, ("ry", "rx"), pairs)


def half_of(w, axis):
    n = w.shape[axis] // 2
    return lax.dynamic_slice_in_dim(w, lax.axis_index("dp") * n, n, axis)


def scatter_row(g, feat):
    return lax.psum_scatter(g, ("ry", "rx", "dp"), scatter_dimension=feat, tiled=True)


class Place:
    def __init__(self):
        self.dp = lax.axis_index("dp")
        self.ry = lax.axis_index("ry")
        self.rx = lax.axis_index("rx")
        self.ch = lax.axis_index("ch")
        self.cl = lax.axis_index("cl")
        self.rows_y = lax.axis_size("ry")
        self.rows = 2 * self.rows_y

    def row_of(self, k):
        return ((self.ry + k // 2) % self.rows_y) * 2 + (self.rx ^ (k % 2))

    def row_from(self, k):
        return ((self.ry - k // 2) % self.rows_y) * 2 + (self.rx ^ (k % 2))

    def slot_from(self, r):
        return ((self.ry - r // 2) % self.rows_y) * 2 + (self.rx ^ (r % 2))

    def both_cores(self, part, feat):
        pair = gather_axis(part, "dp")
        return jnp.concatenate([pair[0], pair[1]], axis=feat).astype(f32)

    def by_tokens(self, got, col, t):
        got = jnp.concatenate(got, axis=0)
        at = lambda c, r: (self.slot_from(r) * 4 + (col ^ c)) * t
        return jnp.concatenate(
            [lax.dynamic_slice_in_dim(got, at(c, r), t, 0) for c in range(4) for r in range(self.rows)], axis=0
        )

    def sum_rows(self, lines):
        pair = lambda y: jnp.concatenate([lines(2 * y), lines(2 * y + 1)], axis=0)
        total = pair(self.ry).astype(f32)
        for j in range(1, self.rows_y):
            total = total + row_send(pair((self.ry + j) % self.rows_y), 2 * j, self.rows).astype(f32)
        n = total.shape[0] // 2
        cut = lambda x: lax.dynamic_slice_in_dim(total, x * n, n, 0)
        return cut(self.rx) + swap(cut(1 - self.rx).astype(bf16), "rx").astype(f32)

    def line_tokens(self, a, col, r, t):
        return jnp.concatenate(
            [lax.dynamic_slice_in_dim(a, ((col ^ k) * self.rows + r) * t, t, 0) for k in range(4)], axis=0
        )

    def exchange(self, *parts):
        got = []
        for k in range(self.rows):
            r = self.row_of(k)
            part = jnp.concatenate([p(r) for p in parts], axis=0) if len(parts) > 1 else parts[0](r)
            got.append(row_send(part, k, self.rows) if k else part)
        return got

    def by_lanes(self, got, lo, hi):
        w = got[0].shape[1]
        got = jnp.concatenate([g[lo:hi] for g in got], axis=1)
        return jnp.concatenate(
            [lax.dynamic_slice_in_dim(got, self.slot_from(r) * w, w, 1) for r in range(self.rows)], axis=1
        )

    def by_rows(self, got, lo, hi):
        n = hi - lo
        got = jnp.concatenate([g[lo:hi] for g in got], axis=0)
        return jnp.concatenate(
            [lax.dynamic_slice_in_dim(got, self.slot_from(r) * n, n, 0) for r in range(self.rows)], axis=0
        )


def multiply(x, w, kind, cost=None):
    def body(x_ref, w_ref, o_ref):
        dot = {"nn": dot_nn, "nt": dot_nt, "tn": dot_tn}[kind]
        o_ref[...] = dot(x_ref[...], w_ref[...]).astype(bf16)

    whole = lambda a: pl.BlockSpec(a.shape, lambda i: (0, 0))
    if kind == "tn":
        m, n, k = x.shape[1], w.shape[1], x.shape[0]
        tile = min(512, m)
        specs = [pl.BlockSpec((k, tile), lambda i: (0, i)), whole(w)]
        out_spec, steps = pl.BlockSpec((tile, n), lambda i: (i, 0)), m // tile
    else:
        m, k = x.shape
        n = w.shape[1] if kind == "nn" else w.shape[0]
        tile = min(512, n)
        by_col, by_row = pl.BlockSpec((k, tile), lambda i: (0, i)), pl.BlockSpec((tile, k), lambda i: (i, 0))
        specs = [whole(x), by_col if kind == "nn" else by_row]
        out_spec, steps = pl.BlockSpec((m, tile), lambda i: (0, i)), n // tile
    return pl.pallas_call(
        body,
        grid=(steps,),
        in_specs=specs,
        out_specs=out_spec,
        out_shape=jax.ShapeDtypeStruct((m, n), bf16),
        compiler_params=pltpu.CompilerParams(
            dimension_semantics=("arbitrary",), vmem_limit_bytes=24 * 1024 * 1024
        ),
        cost_estimate=pl.CostEstimate(
            flops=2 * m * n * k if cost is None else cost,
            bytes_accessed=2 * (m * n + m * k + n * k) if cost is None else cost,
            transcendentals=0,
        ),
    )(x, w)


def feed_forward(x, w, bias, grad_act):
    (m, k), n = x.shape, w.shape[1]
    tile = min(256, n)

    def body(x_ref, w_ref, b_ref, g_ref, a_ref, u_ref):
        u = dot_nn(x_ref[...], w_ref[...]) + b_ref[...]
        square = u * u
        th = jnp.tanh(gelu_a * u * (1.0 + gelu_b * square))
        half = 0.5 * (1.0 + th)
        a_ref[...] = (u * half).astype(bf16)
        slope = half + 0.5 * u * (1.0 - th * th) * (gelu_a + 3.0 * gelu_a * gelu_b * square)
        u_ref[...] = (g_ref[...].astype(f32) * slope).astype(bf16)

    cols = lambda rows: pl.BlockSpec((rows, tile), lambda i: (0, i))
    return pl.pallas_call(
        body,
        grid=(n // tile,),
        in_specs=[pl.BlockSpec((m, k), lambda i: (0, 0)), cols(k), cols(1), cols(m)],
        out_specs=[cols(m), cols(m)],
        out_shape=[jax.ShapeDtypeStruct((m, n), bf16)] * 2,
        compiler_params=pltpu.CompilerParams(
            dimension_semantics=("arbitrary",), vmem_limit_bytes=24 * 1024 * 1024
        ),
        cost_estimate=pl.CostEstimate(
            flops=2 * m * n * k, bytes_accessed=2 * (3 * m * n + m * k + n * k), transcendentals=m * n
        ),
    )(x, w, bias, grad_act)


def stack_heads(a, heads):
    w = a.shape[1] // heads
    return jnp.concatenate([a[:, h * w : (h + 1) * w] for h in range(heads)], axis=0)


def attend_forward(
    bounds, q_ref, k_ref, v_ref, low_ref, pos_ref, o_ref, lse_ref, *, heads, span, scale
):
    chunk = pl.program_id(0)
    rows = stack_heads(q_ref[...], heads)
    n, width = rows.shape
    low = jnp.concatenate([low_ref[0]] * heads, axis=1)
    pos = jnp.concatenate([pos_ref[0]] * heads, axis=1)

    def step(kb, state):
        top, total, acc = state
        start = pl.multiple_of(kb * span, span)
        keys = k_ref[pl.ds(start, span), :]
        values = v_ref[pl.ds(start, span), :]
        s = dot_nt(keys, rows) * scale
        at = start + lax.broadcasted_iota(jnp.int32, (span, n), 0)
        s = jnp.where((at >= low) & (at <= pos), s, negative)
        new = jnp.maximum(top, jnp.max(s, axis=0, keepdims=True))
        p = jnp.exp2(s - new)
        fade = jnp.exp2(top - new)
        total = total * fade + jnp.sum(p, axis=0, keepdims=True)
        acc = acc * fade + dot_tn(values, p.astype(bf16))
        return new, total, acc

    start_state = (
        jnp.full((1, n), negative, f32),
        jnp.zeros((1, n), f32),
        jnp.zeros((width, n), f32),
    )
    top, total, acc = lax.fori_loop(bounds[chunk, 0], bounds[chunk, 1], step, start_state)
    out = (acc / total).T.astype(bf16)
    t = n // heads
    for h in range(heads):
        o_ref[:, h * width : (h + 1) * width] = out[h * t : (h + 1) * t]
    lse_ref[0] = top + jnp.log2(total)


def attend_backward(
    bounds, q_ref, o_ref, g_ref, lse_ref, k_ref, v_ref, low_ref, pos_ref, dq_ref, dkv_ref, *, heads, span, scale, plain
):
    chunk = pl.program_id(0)

    @pl.when(chunk == 0)
    def _():
        dkv_ref[...] = jnp.zeros_like(dkv_ref)

    rows = stack_heads(q_ref[...], heads)
    outs = stack_heads(o_ref[...], heads)
    grads = stack_heads(g_ref[...], heads)
    n, width = rows.shape
    low = jnp.concatenate([low_ref[0]] * heads, axis=1)
    pos = jnp.concatenate([pos_ref[0]] * heads, axis=1)
    lse = lse_ref[0]
    delta = jnp.sum((outs.astype(f32) * grads.astype(f32)).T, axis=0, keepdims=True)

    def step(kb, acc):
        start = pl.multiple_of(kb * span, span)
        keys = k_ref[pl.ds(start, span), :]
        values = v_ref[pl.ds(start, span), :]
        s = dot_nt(keys, rows) * scale
        at = start + lax.broadcasted_iota(jnp.int32, (span, n), 0)
        p = jnp.where((at >= low) & (at <= pos), jnp.exp2(s - lse), 0.0)
        dp = dot_nt(values, grads)
        ds = (p * (dp - delta)).astype(bf16)
        acc = acc + dot_tn(keys, ds)
        dkv_ref[pl.ds(start, span), :width] += dot_nn(ds, rows) * plain
        dkv_ref[pl.ds(start, span), width:] += dot_nn(p.astype(bf16), grads)
        return acc

    acc = lax.fori_loop(bounds[chunk, 0], bounds[chunk, 1], step, jnp.zeros((width, n), f32))
    out = (acc * plain).T.astype(bf16)
    t = n // heads
    for h in range(heads):
        dq_ref[:, h * width : (h + 1) * width] = out[h * t : (h + 1) * t]


class Attention:
    def __init__(self, tokens, chunks, hidden, length, head):
        self.t, self.chunks, self.hidden, self.length, self.head = tokens, chunks, hidden, length, head
        self.heads = hidden // head
        self.span = min(512, length)
        self.plain = head ** (-0.5)
        self.scale = self.plain * log2e
        self.params = pltpu.CompilerParams(
            dimension_semantics=("arbitrary",), vmem_limit_bytes=(20 << 20) + length * 4096
        )
        self.rows_spec = pl.BlockSpec((tokens, hidden), lambda i, b: (i, 0))
        self.kv_spec = pl.BlockSpec((length, head), lambda i, b: (0, 0))
        self.vec_spec = pl.BlockSpec((1, 1, tokens), lambda i, b: (i, 0, 0))
        self.lse_spec = pl.BlockSpec((1, 1, tokens * self.heads), lambda i, b: (i, 0, 0))
        self.cells = tokens * chunks * self.heads * length

    def forward(self, bounds, q, k, v, low, pos):
        body = functools.partial(attend_forward, heads=self.heads, span=self.span, scale=self.scale)
        return pl.pallas_call(
            body,
            grid_spec=pltpu.PrefetchScalarGridSpec(
                num_scalar_prefetch=1,
                grid=(self.chunks,),
                in_specs=[self.rows_spec, self.kv_spec, self.kv_spec, self.vec_spec, self.vec_spec],
                out_specs=[self.rows_spec, self.lse_spec],
            ),
            out_shape=[
                jax.ShapeDtypeStruct(q.shape, bf16),
                jax.ShapeDtypeStruct((self.chunks, 1, self.t * self.heads), f32),
            ],
            compiler_params=self.params,
            cost_estimate=pl.CostEstimate(
                flops=4 * self.cells * self.head, bytes_accessed=4 << 20, transcendentals=self.cells
            ),
        )(bounds, q, k, v, low, pos)

    def backward(self, bounds, q, o, g, lse, k, v, low, pos):
        body = functools.partial(
            attend_backward, heads=self.heads, span=self.span, scale=self.scale, plain=self.plain
        )
        return pl.pallas_call(
            body,
            grid_spec=pltpu.PrefetchScalarGridSpec(
                num_scalar_prefetch=1,
                grid=(self.chunks,),
                in_specs=[self.rows_spec] * 3
                + [self.lse_spec, self.kv_spec, self.kv_spec, self.vec_spec, self.vec_spec],
                out_specs=[
                    self.rows_spec,
                    pl.BlockSpec((self.length, 2 * self.head), lambda i, b: (0, 0)),
                ],
            ),
            out_shape=[
                jax.ShapeDtypeStruct(q.shape, bf16),
                jax.ShapeDtypeStruct((self.length, 2 * self.head), f32),
            ],
            compiler_params=self.params,
            cost_estimate=pl.CostEstimate(
                flops=10 * self.cells * self.head, bytes_accessed=8 << 20, transcendentals=self.cells
            ),
        )(bounds, q, o, g, lse, k, v, low, pos)


def norm_parts(v):
    mean = jnp.mean(v, axis=1, keepdims=True)
    spread = jnp.mean(v * v, axis=1, keepdims=True) - mean * mean
    inv_std = lax.rsqrt(spread + epsilon)
    return (v - mean) * inv_std, inv_std


def norm_back(e, centred, inv_std, gain):
    c = e * gain
    m1 = jnp.mean(c, axis=1, keepdims=True)
    m2 = jnp.mean(c * centred, axis=1, keepdims=True)
    return (c - m1 - centred * m2) * inv_std


gelu_a = math.sqrt(2.0 / math.pi)
gelu_b = 0.044715


def per_device(
    tokens,
    segment_ids,
    ln1_gain,
    ln1_bias,
    w_query,
    b_query,
    w_keyval,
    b_value,
    w_out,
    b_out,
    ln2_gain,
    ln2_bias,
    w_up,
    b_up,
    w_down,
    b_down,
    d_output,
):
    at = Place()
    rows = at.rows
    col_tokens, row_width = tokens.shape
    t = col_tokens // rows
    width = row_width * rows
    head = b_value.shape[0]
    hidden = w_query.shape[1]
    length = segment_ids.shape[1]
    row, col = at.ry * 2 + at.rx, at.ch * 2 + at.cl
    every = ("ry", "rx", "dp")
    rows_of = lambda a, n: lambda r: lax.dynamic_slice_in_dim(a, r * n, n, 0)
    lanes_of = lambda a, n: lambda r: lax.dynamic_slice_in_dim(a, r * n, n, 1)

    gather = lambda w, axis: lax.all_gather(half_of(w, axis), every, axis=axis, tiled=True)
    qkv_weight = gather(jnp.concatenate([w_query, w_keyval], axis=1), 0)
    out_weight = gather(w_out, 1)
    down_weight = gather(w_down, 1)
    up_weight = gather(w_up, 0)

    vectors = jnp.pad(jnp.stack([ln1_gain, ln1_bias, ln2_gain, ln2_bias, b_out, b_down]), ((0, 10), (0, 0)))
    got = at.exchange(rows_of(tokens, t), rows_of(d_output, t), lambda r: vectors)
    got = at.by_lanes(got, 0, got[0].shape[0])
    own, own_grad = got[:t].astype(f32), got[t : 2 * t]
    gain_one, bias_one, gain_two, bias_two, out_bias, down_bias = got[2 * t : 2 * t + 6].astype(f32)[:, None, :]

    segments = segment_ids[0]
    base = jnp.stack([(col ^ k) * col_tokens + row * t for k in range(4)]).astype(jnp.int32)
    pos = base[:, None] + jnp.arange(t, dtype=jnp.int32)[None, :]
    seg_rows = jnp.stack([lax.dynamic_slice_in_dim(segments, base[k], t, 0) for k in range(4)])
    low = jnp.sum((segments[None, None, :] < seg_rows[:, :, None]).astype(jnp.int32), axis=2)
    attention = Attention(t, 4, hidden, length, head)
    span = attention.span
    bounds = jnp.stack([low[:, 0] // span, (base + t - 1) // span + 1], axis=1)
    low, pos = low[:, None, :], pos[:, None, :]

    centred_one, inv_one = norm_parts(own)
    normed_one = (centred_one * gain_one + bias_one).astype(bf16)
    block_one = line_second(normed_one, *line_first(normed_one))
    block_one, own_grad = tie(block_one, own_grad)
    kv_bias = jnp.pad(b_value.astype(f32), (head, 0))
    kv = (dot_nn(block_one, qkv_weight[:, hidden:]) + kv_bias).astype(bf16)
    got = at.exchange(lambda r: kv)
    queries = (dot_nn(block_one, qkv_weight[:, :hidden]) + b_query.astype(f32)).astype(bf16)
    grad_first = line_first(own_grad)
    kv = at.by_tokens(got, col, t)
    keys, values = kv[:, :head], kv[:, head:]
    attended, lse = attention.forward(bounds, queries, keys, values, low, pos)

    part = dot_nn(attended, out_weight).astype(bf16)
    part, grad_first = tie(part, grad_first)
    block_grad = line_second(own_grad, *grad_first)
    end, near, mid = line_scatter_first(part)
    far = line_scatter_second(part, end)
    near, mid, far, block_grad = tie(near, mid, far, block_grad)
    hidden_one = own + out_bias + line_total(part, near, mid, far)
    centred_two, inv_two = norm_parts(hidden_one)
    normed_two = (centred_two * gain_two + bias_two).astype(bf16)
    far, near, mid = line_first(normed_two)
    near, mid, block_grad = tie(near, mid, block_grad)
    grad_act = multiply(block_grad, down_weight, "nt")
    far, grad_act = tie(far, grad_act)
    block_two = line_second(normed_two, far, near, mid)

    activated, grad_upper = feed_forward(block_two, up_weight, b_up.astype(f32)[None, :], grad_act)
    part = multiply(grad_upper, up_weight, "nt")
    part, activated, grad_upper = tie(part, activated, grad_upper)
    end, near, mid = line_scatter_first(part)
    end, mid, activated, grad_upper = tie(end, mid, activated, grad_upper)
    far = line_scatter_second(part, end)
    down_part = multiply(activated, block_grad, "tn", 1)
    up_part = multiply(block_two, grad_upper, "tn", 1)
    near, mid, far, down_part, up_part, activated = tie(near, mid, far, down_part, up_part, activated)
    down_part = scatter_row(down_part, 1)
    up_part = scatter_row(up_part, 0)
    grad_two = line_total(part, near, mid, far)
    grad_hidden = own_grad.astype(f32) + norm_back(grad_two, centred_two, inv_two, gain_two)
    grad_branch = grad_hidden.astype(bf16)
    far, near, mid = line_first(grad_branch)
    near, mid, activated = tie(near, mid, activated)
    final_part = multiply(activated, down_weight, "nn", 1)
    far, final_part = tie(far, final_part)
    block_branch = line_second(grad_branch, far, near, mid)
    grad_att = dot_nt(block_branch, out_weight).astype(bf16)
    grad_att, final_part = tie(grad_att, final_part)
    final_end, final_near, final_mid = line_scatter_first(final_part)
    grad_query, grad_kv = attention.backward(
        bounds, queries, attended, grad_att, lse, keys, values, low, pos
    )

    grad_kv = grad_kv.astype(bf16)
    grad_query, grad_kv, final_end, block_branch, attended = tie(
        grad_query, grad_kv, final_end, block_branch, attended
    )
    part = dot_nt(grad_query, qkv_weight[:, :hidden]).astype(bf16)
    end, near, mid = line_scatter_first(part)
    final_far = line_scatter_second(final_part, final_end)
    kv_grad = at.sum_rows(lambda r: at.line_tokens(grad_kv, col, r, t)).astype(bf16)
    kv_grad, end, grad_query, block_one, down_part, final_far, final_near, final_mid = tie(
        kv_grad, end, grad_query, block_one, down_part, final_far, final_near, final_mid
    )
    far = line_scatter_second(part, end)
    parts = [dot_tn(block_one, grad_query).astype(bf16), dot_tn(block_branch, attended).astype(bf16)]
    shift = lambda a, k: jnp.concatenate([a[(j ^ k) * t : ((j ^ k) + 1) * t] for j in range(4)], axis=0)
    kv_whole = add(kv_grad, shift(swap(kv_grad, "cl"), 1))
    kv_whole = add(kv_whole, shift(swap(kv_whole, "ch"), 2))
    near, mid, far, kv_whole, up_part = tie(near, mid, far, kv_whole, up_part)
    qo_part = scatter_row(jnp.concatenate(parts, axis=1), 0)
    kv_part = dot_tn(kv_whole, block_one).astype(bf16)
    kv_far = swap(lax.dynamic_slice_in_dim(kv_part, (1 - at.dp) * head, head, 0), "dp")
    kv_part = add(half_of(kv_part, 0), kv_far)
    grad_one = line_total(part, near, mid, far) + dot_nt(kv_whole[:t], qkv_weight[:, hidden:])
    grad_own = grad_hidden + norm_back(grad_one, centred_one, inv_one, gain_one)
    final = hidden_one + down_bias + line_total(final_part, final_near, final_mid, final_far)

    sums = lambda a: jnp.sum(a.astype(f32), axis=0)
    tiled = lambda a: jnp.tile(a.reshape(-1, row_width), (1, rows))
    place = lambda a: lax.dynamic_update_slice_in_dim(jnp.zeros((4 * a.shape[0],), f32), a, col * a.shape[0], 0)
    vectors = jnp.stack(
        [
            sums(grad_one * centred_one),
            sums(grad_one),
            sums(grad_two * centred_two),
            sums(grad_two),
            sums(grad_branch),
            sums(own_grad),
        ]
    )
    parts = [
        vectors,
        tiled(jnp.pad(sums(kv_whole[:t, head:]), (0, row_width - head))),
        tiled(place(sums(grad_query))),
        tiled(place(sums(grad_upper))),
    ]
    n = sum(p.shape[0] for p in parts)
    parts.append(jnp.zeros((-n % 16, width), f32))
    packed = jnp.concatenate(parts).astype(bf16)
    n = packed.shape[0]
    got = at.exchange(
        lanes_of(packed, row_width),
        lanes_of(grad_own.astype(bf16), row_width),
        lanes_of(final.astype(bf16), row_width),
        lanes_of(kv_part, row_width),
    )
    total = sum(g[:n].astype(f32) for g in got)
    grad_tokens = at.by_rows(got, n, n + t).astype(f32)
    output = at.by_rows(got, n + t, n + 2 * t)
    kv_part = sum(g[n + 2 * t :].astype(f32) for g in got).astype(bf16)
    grad_w_keyval = gather_axis(kv_part, "dp").reshape(2 * head, row_width).T.astype(f32)
    for axis in ("cl", "ch"):
        total = total.astype(bf16)
        total = total.astype(f32) + swap(total, axis).astype(f32)
    total = total.astype(bf16)
    total = total.astype(f32) + swap(total, "dp").astype(f32)
    grad_w_up = at.both_cores(up_part, 0)
    grad_w_down = at.both_cores(down_part, 1)
    qo_part = at.both_cores(qo_part, 0)
    grad_w_query, grad_w_out = qo_part[:, :hidden], qo_part[:, hidden:].T
    grad_ln1_gain, grad_ln1_bias, grad_ln2_gain, grad_ln2_bias, grad_b_out, grad_b_down = total[:6]
    grad_b_value = total[6, :head]
    of_col = lambda first, n: lax.dynamic_slice_in_dim(
        total[first : first + 4 * n // row_width].reshape(-1), col * n, n, 0
    )
    grad_b_query = of_col(7, hidden)
    grad_b_up = of_col(7 + 4 * hidden // row_width, b_up.shape[0])
    return (
        output,
        grad_tokens,
        grad_ln1_gain,
        grad_ln1_bias,
        grad_w_query,
        grad_b_query,
        grad_w_keyval,
        grad_b_value,
        grad_w_out,
        grad_b_out,
        grad_ln2_gain,
        grad_ln2_bias,
        grad_w_up,
        grad_b_up,
        grad_w_down,
        grad_b_down,
    )


def solution(mesh):
    dp, rows, cols = (mesh.shape[name] for name in ("dp", "row", "col"))
    fine = Mesh(
        mesh.devices.reshape(dp, rows // 2, 2, cols // 2, 2), ("dp", "ry", "rx", "ch", "cl")
    )
    row, col = ("ry", "rx"), ("ch", "cl")
    tok = P(("dp", "ch", "cl"), row)
    in_specs = (
        tok,
        P("dp", None),
        P(row),
        P(row),
        P(row, col),
        P(col),
        P(row, None),
        P(),
        P(col, row),
        P(row),
        P(row),
        P(row),
        P(row, col),
        P(col),
        P(col, row),
        P(row),
        tok,
    )
    out_specs = (
        tok,
        tok,
        P(row),
        P(row),
        P(row, col),
        P(col),
        P(row, None),
        P(),
        P(col, row),
        P(row),
        P(row),
        P(row),
        P(row, col),
        P(col),
        P(col, row),
        P(row),
    )
    return jax.shard_map(
        per_device, mesh=fine, in_specs=in_specs, out_specs=out_specs, check_vma=False
    )
```

```python
import functools
import math

import jax
import jax.numpy as jnp
from jax import lax
from jax.experimental import pallas as pl
from jax.experimental.pallas import tpu as pltpu
from jax.sharding import Mesh
from jax.sharding import PartitionSpec as P

epsilon = 1e-05
negative = -1e30
log2e = math.log2(math.e)
f32 = jnp.float32
bf16 = jnp.bfloat16


def dot_nn(a, b):
    return lax.dot_general(a, b, (((1,), (0,)), ((), ())), preferred_element_type=f32)


def dot_nt(a, b):
    return lax.dot_general(a, b, (((1,), (1,)), ((), ())), preferred_element_type=f32)


def dot_tn(a, b):
    return lax.dot_general(a, b, (((0,), (0,)), ((), ())), preferred_element_type=f32)


def swap(a, axis):
    return lax.ppermute(a, axis, [(0, 1), (1, 0)])


def fetch(a, axis, step):
    n = lax.axis_size(axis)
    return lax.ppermute(a, axis, [(s, (s - step) % n) for s in range(n)])


def tie(*arrays):
    return jax.tree.unflatten(
        jax.tree.structure(arrays), lax.optimization_barrier(tuple(jax.tree.leaves(arrays)))
    )


def add(u, v):
    return (u.astype(f32) + v.astype(f32)).astype(bf16)


def line_first(a):
    return swap(a, "ch"), swap(a, "cl")


def line_second(a, far, near):
    return jnp.concatenate([a, near, far, swap(far, "cl")], axis=0)


def line_scatter_first(p):
    t = p.shape[0] // 4
    return swap(p[3 * t :], "cl"), swap(p[t : 2 * t], "cl")


def line_scatter_second(p, end):
    t = p.shape[0] // 4
    return swap(add(p[2 * t : 3 * t], end), "ch")


def line_total(p, near, far):
    return p[: near.shape[0]].astype(f32) + near.astype(f32) + far.astype(f32)


def gather_axis(a, axis):
    n = lax.axis_size(axis)
    if n == 2:
        b = swap(a, axis)
        first = lax.axis_index(axis) == 0
        return jnp.stack([jnp.where(first, a, b), jnp.where(first, b, a)])
    return lax.all_gather(a, axis, axis=0, tiled=False)


def row_send(a, k, rows):
    n, j, i = rows // 2, k // 2, k % 2
    pairs = [(y * 2 + x, (y + j) % n * 2 + (x ^ i)) for y in range(n) for x in range(2)]
    return lax.ppermute(a, ("ry", "rx"), pairs)


def half_of(w, axis):
    n = w.shape[axis] // 2
    return lax.dynamic_slice_in_dim(w, lax.axis_index("dp") * n, n, axis)


def scatter_row(g, feat):
    return lax.psum_scatter(g, ("ry", "rx"), scatter_dimension=feat, tiled=True)


class Place:
    def __init__(self):
        self.dp = lax.axis_index("dp")
        self.ry = lax.axis_index("ry")
        self.rx = lax.axis_index("rx")
        self.ch = lax.axis_index("ch")
        self.cl = lax.axis_index("cl")
        self.rows_y = lax.axis_size("ry")
        self.rows = 2 * self.rows_y

    def row_of(self, k):
        return ((self.ry + k // 2) % self.rows_y) * 2 + (self.rx ^ (k % 2))

    def row_from(self, k):
        return ((self.ry - k // 2) % self.rows_y) * 2 + (self.rx ^ (k % 2))

    def slot_from(self, r):
        return ((self.ry - r // 2) % self.rows_y) * 2 + (self.rx ^ (r % 2))

    def both_cores(self, part, feat):
        pair = gather_axis(part, "dp")
        return jnp.concatenate([pair[0], pair[1]], axis=feat).astype(f32)

    def by_tokens(self, got, col, t):
        got = jnp.concatenate(got, axis=0)
        at = lambda c, r: (self.slot_from(r) * 4 + (col ^ c)) * t
        return jnp.concatenate(
            [lax.dynamic_slice_in_dim(got, at(c, r), t, 0) for c in range(4) for r in range(self.rows)], axis=0
        )

    def sum_rows(self, lines):
        pair = lambda y: jnp.concatenate([lines(2 * y), lines(2 * y + 1)], axis=0)
        total = pair(self.ry).astype(f32)
        for j in range(1, self.rows_y):
            total = total + row_send(pair((self.ry + j) % self.rows_y), 2 * j, self.rows).astype(f32)
        n = total.shape[0] // 2
        cut = lambda x: lax.dynamic_slice_in_dim(total, x * n, n, 0)
        return cut(self.rx) + swap(cut(1 - self.rx).astype(bf16), "rx").astype(f32)

    def line_tokens(self, a, col, r, t):
        return jnp.concatenate(
            [lax.dynamic_slice_in_dim(a, ((col ^ k) * self.rows + r) * t, t, 0) for k in range(4)], axis=0
        )

    def exchange(self, *parts):
        got = []
        for k in range(self.rows):
            r = self.row_of(k)
            part = jnp.concatenate([p(r) for p in parts], axis=0) if len(parts) > 1 else parts[0](r)
            got.append(row_send(part, k, self.rows) if k else part)
        return got

    def to_tokens(self, a):
        n, w = a.shape[0] // self.rows, a.shape[1]
        cut = lambda y: lax.dynamic_slice_in_dim(a, y * 2 * n, 2 * n, 0)
        got = [cut(self.ry)]
        got += [row_send(cut((self.ry + j) % self.rows_y), 2 * j, self.rows) for j in range(1, self.rows_y)]
        got = jnp.concatenate(got, axis=1)
        part = lambda x: lax.dynamic_slice_in_dim(got, x * n, n, 0)
        got = jnp.concatenate([part(self.rx), swap(part(1 - self.rx), "rx")], axis=1)
        slot = lambda r: ((r % 2) ^ self.rx) * self.rows_y + (self.ry - r // 2) % self.rows_y
        return jnp.concatenate(
            [lax.dynamic_slice_in_dim(got, slot(r) * w, w, 1) for r in range(self.rows)], axis=1
        )

    def to_home(self, a):
        n, w = a.shape[0], a.shape[1] // self.rows
        lanes = lambda x: jnp.concatenate(
            [lax.dynamic_slice_in_dim(a, (2 * y + x) * w, w, 1) for y in range(self.rows_y)], axis=1
        )
        got = jnp.concatenate([lanes(self.rx), swap(lanes(1 - self.rx), "rx")], axis=0)
        cut = lambda y: lax.dynamic_slice_in_dim(got, y * w, w, 1)
        out = [cut(self.ry)]
        out += [row_send(cut((self.ry + j) % self.rows_y), 2 * j, self.rows) for j in range(1, self.rows_y)]
        out = jnp.concatenate(out, axis=0)
        slot = lambda r: (self.ry - r // 2) % self.rows_y * 2 + ((r % 2) ^ self.rx)
        return jnp.concatenate(
            [lax.dynamic_slice_in_dim(out, slot(r) * n, n, 0) for r in range(self.rows)], axis=0
        )

    def by_lanes(self, got, lo, hi):
        w = got[0].shape[1]
        got = jnp.concatenate([g[lo:hi] for g in got], axis=1)
        return jnp.concatenate(
            [lax.dynamic_slice_in_dim(got, self.slot_from(r) * w, w, 1) for r in range(self.rows)], axis=1
        )

    def by_rows(self, got, lo, hi):
        n = hi - lo
        got = jnp.concatenate([g[lo:hi] for g in got], axis=0)
        return jnp.concatenate(
            [lax.dynamic_slice_in_dim(got, self.slot_from(r) * n, n, 0) for r in range(self.rows)], axis=0
        )


def multiply(x, w, kind, cost=None):
    def body(x_ref, w_ref, o_ref):
        dot = {"nn": dot_nn, "nt": dot_nt, "tn": dot_tn}[kind]
        o_ref[...] = dot(x_ref[...], w_ref[...]).astype(bf16)

    whole = lambda a: pl.BlockSpec(a.shape, lambda i: (0, 0))
    if kind == "tn":
        m, n, k = x.shape[1], w.shape[1], x.shape[0]
        tile = min(512, m)
        specs = [pl.BlockSpec((k, tile), lambda i: (0, i)), whole(w)]
        out_spec, steps = pl.BlockSpec((tile, n), lambda i: (i, 0)), m // tile
    else:
        m, k = x.shape
        n = w.shape[1] if kind == "nn" else w.shape[0]
        tile = min(512, n)
        by_col, by_row = pl.BlockSpec((k, tile), lambda i: (0, i)), pl.BlockSpec((tile, k), lambda i: (i, 0))
        specs = [whole(x), by_col if kind == "nn" else by_row]
        out_spec, steps = pl.BlockSpec((m, tile), lambda i: (0, i)), n // tile
    return pl.pallas_call(
        body,
        grid=(steps,),
        in_specs=specs,
        out_specs=out_spec,
        out_shape=jax.ShapeDtypeStruct((m, n), bf16),
        compiler_params=pltpu.CompilerParams(
            dimension_semantics=("arbitrary",), vmem_limit_bytes=24 * 1024 * 1024
        ),
        cost_estimate=pl.CostEstimate(
            flops=2 * m * n * k if cost is None else cost,
            bytes_accessed=2 * (m * n + m * k + n * k) if cost is None else cost,
            transcendentals=0,
        ),
    )(x, w)


def feed_forward(x, w, bias, grad_act):
    (m, k), n = x.shape, w.shape[1]
    tile = min(256, n)

    def body(x_ref, w_ref, b_ref, g_ref, a_ref, u_ref):
        u = dot_nn(x_ref[...], w_ref[...]) + b_ref[...]
        square = u * u
        th = jnp.tanh(gelu_a * u * (1.0 + gelu_b * square))
        half = 0.5 * (1.0 + th)
        a_ref[...] = (u * half).astype(bf16)
        slope = half + 0.5 * u * (1.0 - th * th) * (gelu_a + 3.0 * gelu_a * gelu_b * square)
        u_ref[...] = (g_ref[...].astype(f32) * slope).astype(bf16)

    cols = lambda rows: pl.BlockSpec((rows, tile), lambda i: (0, i))
    return pl.pallas_call(
        body,
        grid=(n // tile,),
        in_specs=[pl.BlockSpec((m, k), lambda i: (0, 0)), cols(k), cols(1), cols(m)],
        out_specs=[cols(m), cols(m)],
        out_shape=[jax.ShapeDtypeStruct((m, n), bf16)] * 2,
        compiler_params=pltpu.CompilerParams(
            dimension_semantics=("arbitrary",), vmem_limit_bytes=24 * 1024 * 1024
        ),
        cost_estimate=pl.CostEstimate(
            flops=2 * m * n * k, bytes_accessed=2 * (3 * m * n + m * k + n * k), transcendentals=m * n
        ),
    )(x, w, bias, grad_act)


def outer(half, x, y, split, more=None):
    k, m, n = x.shape[0], x.shape[1], y.shape[1]
    m, n = (m // 2, n) if split == 0 else (m, n // 2)
    tile = min(512, m)
    steps = m // tile

    def body(half_ref, x_ref, y_ref, *refs):
        total = dot_tn(x_ref[...], y_ref[...])
        if more is not None:
            total = total + refs[0][...].astype(f32)
        refs[-1][...] = total.astype(bf16)

    out = pl.BlockSpec((tile, n), lambda i, half: (i, 0))
    first = (lambda i, half: (0, half[0] * steps + i)) if split == 0 else (lambda i, half: (0, i))
    second = (lambda i, half: (0, 0)) if split == 0 else (lambda i, half: (0, half[0]))
    args = (x, y) if more is None else (x, y, more)
    return pl.pallas_call(
        body,
        grid_spec=pltpu.PrefetchScalarGridSpec(
            num_scalar_prefetch=1,
            grid=(steps,),
            in_specs=[pl.BlockSpec((k, tile), first), pl.BlockSpec((k, n), second)]
            + [out] * (more is not None),
            out_specs=out,
        ),
        out_shape=jax.ShapeDtypeStruct((m, n), bf16),
        compiler_params=pltpu.CompilerParams(
            dimension_semantics=("arbitrary",), vmem_limit_bytes=24 * 1024 * 1024
        ),
        cost_estimate=pl.CostEstimate(flops=1, bytes_accessed=1, transcendentals=0),
    )(half, *args)


def stack_heads(a, heads):
    w = a.shape[1] // heads
    return jnp.concatenate([a[:, h * w : (h + 1) * w] for h in range(heads)], axis=0)


def attend_forward(
    bounds, q_ref, k_ref, v_ref, low_ref, pos_ref, o_ref, lse_ref, *, heads, span, scale
):
    chunk = pl.program_id(0)
    rows = stack_heads(q_ref[...], heads)
    n, width = rows.shape
    low = jnp.concatenate([low_ref[0]] * heads, axis=1)
    pos = jnp.concatenate([pos_ref[0]] * heads, axis=1)

    def step(kb, state):
        top, total, acc = state
        start = pl.multiple_of(kb * span, span)
        keys = k_ref[pl.ds(start, span), :]
        values = v_ref[pl.ds(start, span), :]
        s = dot_nt(keys, rows) * scale
        at = start + lax.broadcasted_iota(jnp.int32, (span, n), 0)
        s = jnp.where((at >= low) & (at <= pos), s, negative)
        new = jnp.maximum(top, jnp.max(s, axis=0, keepdims=True))
        p = jnp.exp2(s - new)
        fade = jnp.exp2(top - new)
        total = total * fade + jnp.sum(p, axis=0, keepdims=True)
        acc = acc * fade + dot_tn(values, p.astype(bf16))
        return new, total, acc

    start_state = (
        jnp.full((1, n), negative, f32),
        jnp.zeros((1, n), f32),
        jnp.zeros((width, n), f32),
    )
    top, total, acc = lax.fori_loop(bounds[chunk, 0], bounds[chunk, 1], step, start_state)
    out = (acc / total).T.astype(bf16)
    t = n // heads
    for h in range(heads):
        o_ref[:, h * width : (h + 1) * width] = out[h * t : (h + 1) * t]
    lse_ref[0] = top + jnp.log2(total)


def attend_backward(
    bounds, q_ref, o_ref, g_ref, lse_ref, k_ref, v_ref, low_ref, pos_ref, dq_ref, dkv_ref, *, heads, span, scale, plain
):
    chunk = pl.program_id(0)

    @pl.when(chunk == 0)
    def _():
        dkv_ref[...] = jnp.zeros_like(dkv_ref)

    rows = stack_heads(q_ref[...], heads)
    outs = stack_heads(o_ref[...], heads)
    grads = stack_heads(g_ref[...], heads)
    n, width = rows.shape
    low = jnp.concatenate([low_ref[0]] * heads, axis=1)
    pos = jnp.concatenate([pos_ref[0]] * heads, axis=1)
    lse = lse_ref[0]
    delta = jnp.sum((outs.astype(f32) * grads.astype(f32)).T, axis=0, keepdims=True)

    def step(kb, acc):
        start = pl.multiple_of(kb * span, span)
        keys = k_ref[pl.ds(start, span), :]
        values = v_ref[pl.ds(start, span), :]
        s = dot_nt(keys, rows) * scale
        at = start + lax.broadcasted_iota(jnp.int32, (span, n), 0)
        p = jnp.where((at >= low) & (at <= pos), jnp.exp2(s - lse), 0.0)
        dp = dot_nt(values, grads)
        ds = (p * (dp - delta)).astype(bf16)
        acc = acc + dot_tn(keys, ds)
        dkv_ref[pl.ds(start, span), :width] += dot_nn(ds, rows) * plain
        dkv_ref[pl.ds(start, span), width:] += dot_nn(p.astype(bf16), grads)
        return acc

    acc = lax.fori_loop(bounds[chunk, 0], bounds[chunk, 1], step, jnp.zeros((width, n), f32))
    out = (acc * plain).T.astype(bf16)
    t = n // heads
    for h in range(heads):
        dq_ref[:, h * width : (h + 1) * width] = out[h * t : (h + 1) * t]


class Attention:
    def __init__(self, tokens, chunks, hidden, length, head):
        self.t, self.chunks, self.hidden, self.length, self.head = tokens, chunks, hidden, length, head
        self.heads = hidden // head
        self.span = min(512, length)
        self.plain = head ** (-0.5)
        self.scale = self.plain * log2e
        self.params = pltpu.CompilerParams(
            dimension_semantics=("arbitrary",), vmem_limit_bytes=(20 << 20) + length * 4096
        )
        self.rows_spec = pl.BlockSpec((tokens, hidden), lambda i, b: (i, 0))
        self.kv_spec = pl.BlockSpec((length, head), lambda i, b: (0, 0))
        self.vec_spec = pl.BlockSpec((1, 1, tokens), lambda i, b: (i, 0, 0))
        self.lse_spec = pl.BlockSpec((1, 1, tokens * self.heads), lambda i, b: (i, 0, 0))
        self.cells = tokens * chunks * self.heads * length

    def forward(self, bounds, q, k, v, low, pos):
        body = functools.partial(attend_forward, heads=self.heads, span=self.span, scale=self.scale)
        return pl.pallas_call(
            body,
            grid_spec=pltpu.PrefetchScalarGridSpec(
                num_scalar_prefetch=1,
                grid=(self.chunks,),
                in_specs=[self.rows_spec, self.kv_spec, self.kv_spec, self.vec_spec, self.vec_spec],
                out_specs=[self.rows_spec, self.lse_spec],
            ),
            out_shape=[
                jax.ShapeDtypeStruct(q.shape, bf16),
                jax.ShapeDtypeStruct((self.chunks, 1, self.t * self.heads), f32),
            ],
            compiler_params=self.params,
            cost_estimate=pl.CostEstimate(
                flops=4 * self.cells * self.head, bytes_accessed=4 << 20, transcendentals=self.cells
            ),
        )(bounds, q, k, v, low, pos)

    def backward(self, bounds, q, o, g, lse, k, v, low, pos):
        body = functools.partial(
            attend_backward, heads=self.heads, span=self.span, scale=self.scale, plain=self.plain
        )
        return pl.pallas_call(
            body,
            grid_spec=pltpu.PrefetchScalarGridSpec(
                num_scalar_prefetch=1,
                grid=(self.chunks,),
                in_specs=[self.rows_spec] * 3
                + [self.lse_spec, self.kv_spec, self.kv_spec, self.vec_spec, self.vec_spec],
                out_specs=[
                    self.rows_spec,
                    pl.BlockSpec((self.length, 2 * self.head), lambda i, b: (0, 0)),
                ],
            ),
            out_shape=[
                jax.ShapeDtypeStruct(q.shape, bf16),
                jax.ShapeDtypeStruct((self.length, 2 * self.head), f32),
            ],
            compiler_params=self.params,
            cost_estimate=pl.CostEstimate(
                flops=10 * self.cells * self.head, bytes_accessed=8 << 20, transcendentals=self.cells
            ),
        )(bounds, q, o, g, lse, k, v, low, pos)


def norm_parts(v):
    mean = jnp.mean(v, axis=1, keepdims=True)
    spread = jnp.mean(v * v, axis=1, keepdims=True) - mean * mean
    inv_std = lax.rsqrt(spread + epsilon)
    return (v - mean) * inv_std, inv_std


def norm_back(e, centred, inv_std, gain):
    c = e * gain
    m1 = jnp.mean(c, axis=1, keepdims=True)
    m2 = jnp.mean(c * centred, axis=1, keepdims=True)
    return (c - m1 - centred * m2) * inv_std


gelu_a = math.sqrt(2.0 / math.pi)
gelu_b = 0.044715


def per_device(
    tokens,
    segment_ids,
    ln1_gain,
    ln1_bias,
    w_query,
    b_query,
    w_keyval,
    b_value,
    w_out,
    b_out,
    ln2_gain,
    ln2_bias,
    w_up,
    b_up,
    w_down,
    b_down,
    d_output,
):
    at = Place()
    rows = at.rows
    col_tokens, row_width = tokens.shape
    t = col_tokens // rows
    width = row_width * rows
    head = b_value.shape[0]
    hidden = w_query.shape[1]
    length = segment_ids.shape[1]
    row, col = at.ry * 2 + at.rx, at.ch * 2 + at.cl
    every = ("ry", "rx", "dp")
    rows_of = lambda a, n: lambda r: lax.dynamic_slice_in_dim(a, r * n, n, 0)
    lanes_of = lambda a, n: lambda r: lax.dynamic_slice_in_dim(a, r * n, n, 1)

    gather = lambda w, axis: lax.all_gather(half_of(w, axis), every, axis=axis, tiled=True)
    qkvo_weight = gather(jnp.concatenate([w_query, w_keyval, w_out.T], axis=1), 0)
    qkv_weight, out_weight = qkvo_weight[:, : hidden + 2 * head], qkvo_weight[:, hidden + 2 * head :]
    down_weight = gather(w_down, 1)
    up_weight = gather(w_up, 0)

    vectors = jnp.pad(jnp.stack([ln1_gain, ln1_bias, ln2_gain, ln2_bias, b_out, b_down]), ((0, 10), (0, 0)))
    got = at.exchange(rows_of(tokens, t), lambda r: vectors)
    got = at.by_lanes(got, 0, got[0].shape[0])
    got, d_output = tie(got, d_output)
    own = got[:t].astype(f32)
    gain_one, bias_one, gain_two, bias_two, out_bias, down_bias = got[t : t + 6].astype(f32)[:, None, :]
    own_grad = at.to_tokens(d_output)

    segments = segment_ids[0]
    base = jnp.stack([(col ^ k) * col_tokens + row * t for k in range(4)]).astype(jnp.int32)
    pos = base[:, None] + jnp.arange(t, dtype=jnp.int32)[None, :]
    seg_rows = jnp.stack([lax.dynamic_slice_in_dim(segments, base[k], t, 0) for k in range(4)])
    low = jnp.sum((segments[None, None, :] < seg_rows[:, :, None]).astype(jnp.int32), axis=2)
    attention = Attention(t, 4, hidden, length, head)
    span = attention.span
    bounds = jnp.stack([low[:, 0] // span, (base + t - 1) // span + 1], axis=1)
    low, pos = low[:, None, :], pos[:, None, :]

    centred_one, inv_one = norm_parts(own)
    normed_one = (centred_one * gain_one + bias_one).astype(bf16)
    block_one = line_second(normed_one, *tie(*line_first(normed_one)))
    block_one, own_grad = tie(block_one, own_grad)
    kv_bias = jnp.pad(b_value.astype(f32), (head, 0))
    kv = (dot_nn(block_one, qkv_weight[:, hidden:]) + kv_bias).astype(bf16)
    got = at.exchange(lambda r: kv)
    queries = (dot_nn(block_one, qkv_weight[:, :hidden]) + b_query.astype(f32)).astype(bf16)
    grad_first = line_first(own_grad)
    kv = at.by_tokens(got, col, t)
    keys, values = kv[:, :head], kv[:, head:]
    attended, lse = attention.forward(bounds, queries, keys, values, low, pos)

    part = dot_nt(attended, out_weight).astype(bf16)
    part, grad_first = tie(part, grad_first)
    block_grad = line_second(own_grad, *grad_first)
    end, near = line_scatter_first(part)
    far = line_scatter_second(part, end)
    near, far, block_grad = tie(near, far, block_grad)
    hidden_one = own + out_bias + line_total(part, near, far)
    centred_two, inv_two = norm_parts(hidden_one)
    normed_two = (centred_two * gain_two + bias_two).astype(bf16)
    far, near = line_first(normed_two)
    grad_act = multiply(block_grad, down_weight, "nt")
    far, near, grad_act = tie(far, near, grad_act)
    block_two = line_second(normed_two, far, near)

    core = at.dp.astype(jnp.int32).reshape(1)
    activated, grad_upper = feed_forward(block_two, up_weight, b_up.astype(f32)[None, :], grad_act)
    part = multiply(grad_upper, up_weight, "nt")
    part, activated, grad_upper = tie(part, activated, grad_upper)
    end, near = line_scatter_first(part)
    down_part = outer(1 - core, activated, block_grad, 0)
    up_part = outer(1 - core, block_two, grad_upper, 1)
    end, down_part, up_part, activated, grad_upper = tie(end, down_part, up_part, activated, grad_upper)
    far = line_scatter_second(part, end)
    down_part, up_part = swap(down_part, "dp"), swap(up_part, "dp")
    down_part = outer(core, activated, block_grad, 0, down_part)
    up_part = outer(core, block_two, grad_upper, 1, up_part)
    near, far, down_part, up_part, activated = tie(near, far, down_part, up_part, activated)
    down_part = scatter_row(down_part, 1)
    up_part = scatter_row(up_part, 0)
    grad_two = line_total(part, near, far)
    grad_hidden = own_grad.astype(f32) + norm_back(grad_two, centred_two, inv_two, gain_two)
    grad_branch = grad_hidden.astype(bf16)
    far, near = line_first(grad_branch)
    far, near, activated = tie(far, near, activated)
    block_branch = line_second(grad_branch, far, near)
    grad_att = dot_nn(block_branch, out_weight).astype(bf16)
    grad_query, grad_kv = attention.backward(
        bounds, queries, attended, grad_att, lse, keys, values, low, pos
    )

    grad_kv = grad_kv.astype(bf16)
    grad_query, grad_kv, block_branch, attended, activated = tie(
        grad_query, grad_kv, block_branch, attended, activated
    )
    final_part = multiply(activated, down_weight, "nn", 1)
    part = dot_nt(grad_query, qkv_weight[:, :hidden]).astype(bf16)
    end, near = line_scatter_first(part)
    kv_grad = at.sum_rows(lambda r: at.line_tokens(grad_kv, col, r, t)).astype(bf16)
    far = line_scatter_second(part, end)
    kv_grad, grad_query, block_one, down_part = tie(kv_grad, grad_query, block_one, down_part)
    parts = [dot_tn(block_one, grad_query).astype(bf16), dot_tn(block_branch, attended).astype(bf16)]
    qo_part = jnp.concatenate(parts, axis=1)
    cut = lambda k: kv_grad[k * t : (k + 1) * t]
    got = swap(jnp.concatenate([cut(1), cut(3)], axis=0), "cl")
    got, final_part = tie(got, final_part)
    kv_own = add(add(cut(0), got[:t]), swap(add(cut(2), got[t:]), "ch"))
    final_end, final_near = line_scatter_first(final_part)
    grad_w_down = at.both_cores(down_part, 0)
    kv_part = dot_tn(kv_own, normed_one).astype(bf16)
    kv_far = swap(lax.dynamic_slice_in_dim(kv_part, (1 - at.dp) * head, head, 0), "dp")
    kv_part = add(half_of(kv_part, 0), kv_far)
    near, far, kv_own, kv_part, up_part, qo_part, final_end, grad_w_down = tie(
        near, far, kv_own, kv_part, up_part, qo_part, final_end, grad_w_down
    )
    final_far = line_scatter_second(final_part, final_end)
    qo_part = lax.psum_scatter(qo_part, ("ry", "rx", "dp"), scatter_dimension=0, tiled=True)
    grad_one = line_total(part, near, far) + dot_nt(kv_own, qkv_weight[:, hidden:])
    grad_own = grad_hidden + norm_back(grad_one, centred_one, inv_one, gain_one)

    sums = lambda a: jnp.sum(a.astype(f32), axis=0)
    tiled = lambda a: jnp.tile(a.reshape(-1, row_width), (1, rows))
    place = lambda a: lax.dynamic_update_slice_in_dim(jnp.zeros((4 * a.shape[0],), f32), a, col * a.shape[0], 0)
    vectors = jnp.stack(
        [
            sums(grad_one * centred_one),
            sums(grad_one),
            sums(grad_two * centred_two),
            sums(grad_two),
            sums(grad_branch),
            sums(own_grad),
        ]
    )
    parts = [
        vectors,
        tiled(jnp.pad(sums(kv_own[:, head:]), (0, row_width - head))),
        tiled(place(sums(grad_query))),
        tiled(place(sums(grad_upper))),
    ]
    n = sum(p.shape[0] for p in parts)
    parts.append(jnp.zeros((-n % 16, width), f32))
    packed = jnp.concatenate(parts).astype(bf16)
    n = packed.shape[0]
    packed = jnp.concatenate([packed, kv_part], axis=0)
    got = at.exchange(lanes_of(packed, row_width), lanes_of(grad_own.astype(bf16), row_width))
    total = sum(g[: n + head].astype(f32) for g in got)
    grad_tokens = at.by_rows(got, n + head, n + head + t).astype(f32)
    total, final_near, final_far = tie(total, final_near, final_far)
    final = hidden_one + down_bias + line_total(final_part, final_near, final_far)
    output = at.to_home(final.astype(bf16))
    for axis in ("cl", "ch"):
        total = total.astype(bf16)
        total = total.astype(f32) + swap(total, axis).astype(f32)
    total = gather_axis(total.astype(bf16), "dp").astype(f32)
    grad_w_keyval = total[:, n:].reshape(2 * head, row_width).T
    total = total[0, :n] + total[1, :n]
    qo_part = at.both_cores(qo_part, 0)
    grad_w_query, grad_w_out = qo_part[:, :hidden], qo_part[:, hidden:].T
    grad_w_up = at.both_cores(up_part, 1)
    grad_ln1_gain, grad_ln1_bias, grad_ln2_gain, grad_ln2_bias, grad_b_out, grad_b_down = total[:6]
    grad_b_value = total[6, :head]
    of_col = lambda first, n: lax.dynamic_slice_in_dim(
        total[first : first + 4 * n // row_width].reshape(-1), col * n, n, 0
    )
    grad_b_query = of_col(7, hidden)
    grad_b_up = of_col(7 + 4 * hidden // row_width, b_up.shape[0])
    return (
        output,
        grad_tokens,
        grad_ln1_gain,
        grad_ln1_bias,
        grad_w_query,
        grad_b_query,
        grad_w_keyval,
        grad_b_value,
        grad_w_out,
        grad_b_out,
        grad_ln2_gain,
        grad_ln2_bias,
        grad_w_up,
        grad_b_up,
        grad_w_down,
        grad_b_down,
    )


def solution(mesh):
    dp, rows, cols = (mesh.shape[name] for name in ("dp", "row", "col"))
    fine = Mesh(
        mesh.devices.reshape(dp, rows // 2, 2, cols // 2, 2), ("dp", "ry", "rx", "ch", "cl")
    )
    row, col = ("ry", "rx"), ("ch", "cl")
    tok = P(("dp", "ch", "cl"), row)
    in_specs = (
        tok,
        P("dp", None),
        P(row),
        P(row),
        P(row, col),
        P(col),
        P(row, None),
        P(),
        P(col, row),
        P(row),
        P(row),
        P(row),
        P(row, col),
        P(col),
        P(col, row),
        P(row),
        tok,
    )
    out_specs = (
        tok,
        tok,
        P(row),
        P(row),
        P(row, col),
        P(col),
        P(row, None),
        P(),
        P(col, row),
        P(row),
        P(row),
        P(row),
        P(row, col),
        P(col),
        P(col, row),
        P(row),
    )
    return jax.shard_map(
        per_device, mesh=fine, in_specs=in_specs, out_specs=out_specs, check_vma=False
    )
```

```python
import functools
import math

import jax
import jax.numpy as jnp
from jax import lax
from jax.experimental import pallas as pl
from jax.experimental.pallas import tpu as pltpu
from jax.sharding import Mesh
from jax.sharding import PartitionSpec as P

epsilon = 1e-05
negative = -1e30
log2e = math.log2(math.e)
f32 = jnp.float32
bf16 = jnp.bfloat16


def dot_nn(a, b):
    return lax.dot_general(a, b, (((1,), (0,)), ((), ())), preferred_element_type=f32)


def dot_nt(a, b):
    return lax.dot_general(a, b, (((1,), (1,)), ((), ())), preferred_element_type=f32)


def dot_tn(a, b):
    return lax.dot_general(a, b, (((0,), (0,)), ((), ())), preferred_element_type=f32)


def swap(a, axis):
    return lax.ppermute(a, axis, [(0, 1), (1, 0)])


def fetch(a, axis, step):
    n = lax.axis_size(axis)
    return lax.ppermute(a, axis, [(s, (s - step) % n) for s in range(n)])


def tie(*arrays):
    return jax.tree.unflatten(
        jax.tree.structure(arrays), lax.optimization_barrier(tuple(jax.tree.leaves(arrays)))
    )


def add(u, v):
    return (u.astype(f32) + v.astype(f32)).astype(bf16)


def line_first(a):
    return swap(a, "ch"), swap(a, "cl")


def line_second(a, far, near):
    return jnp.concatenate([a, near, far, swap(far, "cl")], axis=0)


def line_scatter_first(p):
    t = p.shape[0] // 4
    return swap(p[3 * t :], "cl"), swap(p[t : 2 * t], "cl")


def line_scatter_second(p, end):
    t = p.shape[0] // 4
    return swap(add(p[2 * t : 3 * t], end), "ch")


def line_total(p, near, far):
    return p[: near.shape[0]].astype(f32) + near.astype(f32) + far.astype(f32)


def gather_axis(a, axis):
    n = lax.axis_size(axis)
    if n == 2:
        b = swap(a, axis)
        first = lax.axis_index(axis) == 0
        return jnp.stack([jnp.where(first, a, b), jnp.where(first, b, a)])
    return lax.all_gather(a, axis, axis=0, tiled=False)


def row_send(a, k, rows):
    n, j, i = rows // 2, k // 2, k % 2
    pairs = [(y * 2 + x, (y + j) % n * 2 + (x ^ i)) for y in range(n) for x in range(2)]
    return lax.ppermute(a, ("ry", "rx"), pairs)


def half_of(w, axis):
    n = w.shape[axis] // 2
    return lax.dynamic_slice_in_dim(w, lax.axis_index("dp") * n, n, axis)


def scatter_row(g, feat):
    return lax.psum_scatter(g, ("ry", "rx"), scatter_dimension=feat, tiled=True)


class Place:
    def __init__(self):
        self.dp = lax.axis_index("dp")
        self.ry = lax.axis_index("ry")
        self.rx = lax.axis_index("rx")
        self.ch = lax.axis_index("ch")
        self.cl = lax.axis_index("cl")
        self.rows_y = lax.axis_size("ry")
        self.rows = 2 * self.rows_y

    def row_of(self, k):
        return ((self.ry + k // 2) % self.rows_y) * 2 + (self.rx ^ (k % 2))

    def row_from(self, k):
        return ((self.ry - k // 2) % self.rows_y) * 2 + (self.rx ^ (k % 2))

    def slot_from(self, r):
        return ((self.ry - r // 2) % self.rows_y) * 2 + (self.rx ^ (r % 2))

    def both_cores(self, part, feat):
        pair = gather_axis(part, "dp")
        return jnp.concatenate([pair[0], pair[1]], axis=feat).astype(f32)

    def by_tokens(self, got, col, t):
        got = jnp.concatenate(got, axis=0)
        at = lambda c, r: (self.slot_from(r) * 4 + (col ^ c)) * t
        return jnp.concatenate(
            [lax.dynamic_slice_in_dim(got, at(c, r), t, 0) for c in range(4) for r in range(self.rows)], axis=0
        )

    def sum_rows(self, lines):
        pair = lambda y: jnp.concatenate([lines(2 * y), lines(2 * y + 1)], axis=0)
        total = pair(self.ry).astype(f32)
        for j in range(1, self.rows_y):
            total = total + row_send(pair((self.ry + j) % self.rows_y), 2 * j, self.rows).astype(f32)
        n = total.shape[0] // 2
        cut = lambda x: lax.dynamic_slice_in_dim(total, x * n, n, 0)
        return cut(self.rx) + swap(cut(1 - self.rx).astype(bf16), "rx").astype(f32)

    def line_tokens(self, a, col, r, t):
        return jnp.concatenate(
            [lax.dynamic_slice_in_dim(a, ((col ^ k) * self.rows + r) * t, t, 0) for k in range(4)], axis=0
        )

    def exchange(self, *parts):
        got = []
        for k in range(self.rows):
            r = self.row_of(k)
            part = jnp.concatenate([p(r) for p in parts], axis=0) if len(parts) > 1 else parts[0](r)
            got.append(row_send(part, k, self.rows) if k else part)
        return got

    def to_tokens(self, a):
        n, w = a.shape[0] // self.rows, a.shape[1]
        cut = lambda y: lax.dynamic_slice_in_dim(a, y * 2 * n, 2 * n, 0)
        got = [cut(self.ry)]
        got += [row_send(cut((self.ry + j) % self.rows_y), 2 * j, self.rows) for j in range(1, self.rows_y)]
        got = jnp.concatenate(got, axis=1)
        part = lambda x: lax.dynamic_slice_in_dim(got, x * n, n, 0)
        got = jnp.concatenate([part(self.rx), swap(part(1 - self.rx), "rx")], axis=1)
        slot = lambda r: ((r % 2) ^ self.rx) * self.rows_y + (self.ry - r // 2) % self.rows_y
        return jnp.concatenate(
            [lax.dynamic_slice_in_dim(got, slot(r) * w, w, 1) for r in range(self.rows)], axis=1
        )

    def by_lanes(self, got, lo, hi):
        w = got[0].shape[1]
        got = jnp.concatenate([g[lo:hi] for g in got], axis=1)
        return jnp.concatenate(
            [lax.dynamic_slice_in_dim(got, self.slot_from(r) * w, w, 1) for r in range(self.rows)], axis=1
        )

    def by_rows(self, got, lo, hi):
        n = hi - lo
        got = jnp.concatenate([g[lo:hi] for g in got], axis=0)
        return jnp.concatenate(
            [lax.dynamic_slice_in_dim(got, self.slot_from(r) * n, n, 0) for r in range(self.rows)], axis=0
        )


def multiply(x, w, kind, cost=None):
    def body(x_ref, w_ref, o_ref):
        dot = {"nn": dot_nn, "nt": dot_nt, "tn": dot_tn}[kind]
        o_ref[...] = dot(x_ref[...], w_ref[...]).astype(bf16)

    whole = lambda a: pl.BlockSpec(a.shape, lambda i: (0, 0))
    if kind == "tn":
        m, n, k = x.shape[1], w.shape[1], x.shape[0]
        tile = min(512, m)
        specs = [pl.BlockSpec((k, tile), lambda i: (0, i)), whole(w)]
        out_spec, steps = pl.BlockSpec((tile, n), lambda i: (i, 0)), m // tile
    else:
        m, k = x.shape
        n = w.shape[1] if kind == "nn" else w.shape[0]
        tile = min(512, n)
        by_col, by_row = pl.BlockSpec((k, tile), lambda i: (0, i)), pl.BlockSpec((tile, k), lambda i: (i, 0))
        specs = [whole(x), by_col if kind == "nn" else by_row]
        out_spec, steps = pl.BlockSpec((m, tile), lambda i: (0, i)), n // tile
    return pl.pallas_call(
        body,
        grid=(steps,),
        in_specs=specs,
        out_specs=out_spec,
        out_shape=jax.ShapeDtypeStruct((m, n), bf16),
        compiler_params=pltpu.CompilerParams(
            dimension_semantics=("arbitrary",), vmem_limit_bytes=24 * 1024 * 1024
        ),
        cost_estimate=pl.CostEstimate(
            flops=2 * m * n * k if cost is None else cost,
            bytes_accessed=2 * (m * n + m * k + n * k) if cost is None else cost,
            transcendentals=0,
        ),
    )(x, w)


def feed_forward(x, w, bias, grad_act):
    (m, k), n = x.shape, w.shape[1]
    tile = min(256, n)

    def body(x_ref, w_ref, b_ref, g_ref, a_ref, u_ref):
        u = dot_nn(x_ref[...], w_ref[...]) + b_ref[...]
        square = u * u
        th = jnp.tanh(gelu_a * u * (1.0 + gelu_b * square))
        half = 0.5 * (1.0 + th)
        a_ref[...] = (u * half).astype(bf16)
        slope = half + 0.5 * u * (1.0 - th * th) * (gelu_a + 3.0 * gelu_a * gelu_b * square)
        u_ref[...] = (g_ref[...].astype(f32) * slope).astype(bf16)

    cols = lambda rows: pl.BlockSpec((rows, tile), lambda i: (0, i))
    return pl.pallas_call(
        body,
        grid=(n // tile,),
        in_specs=[pl.BlockSpec((m, k), lambda i: (0, 0)), cols(k), cols(1), cols(m)],
        out_specs=[cols(m), cols(m)],
        out_shape=[jax.ShapeDtypeStruct((m, n), bf16)] * 2,
        compiler_params=pltpu.CompilerParams(
            dimension_semantics=("arbitrary",), vmem_limit_bytes=24 * 1024 * 1024
        ),
        cost_estimate=pl.CostEstimate(
            flops=2 * m * n * k, bytes_accessed=2 * (3 * m * n + m * k + n * k), transcendentals=m * n
        ),
    )(x, w, bias, grad_act)


def outer(half, x, y, split, more=None):
    k, m, n = x.shape[0], x.shape[1], y.shape[1]
    m, n = (m // 2, n) if split == 0 else (m, n // 2)
    tile = min(512, m)
    steps = m // tile

    def body(half_ref, x_ref, y_ref, *refs):
        total = dot_tn(x_ref[...], y_ref[...])
        if more is not None:
            total = total + refs[0][...].astype(f32)
        refs[-1][...] = total.astype(bf16)

    out = pl.BlockSpec((tile, n), lambda i, half: (i, 0))
    first = (lambda i, half: (0, half[0] * steps + i)) if split == 0 else (lambda i, half: (0, i))
    second = (lambda i, half: (0, 0)) if split == 0 else (lambda i, half: (0, half[0]))
    args = (x, y) if more is None else (x, y, more)
    return pl.pallas_call(
        body,
        grid_spec=pltpu.PrefetchScalarGridSpec(
            num_scalar_prefetch=1,
            grid=(steps,),
            in_specs=[pl.BlockSpec((k, tile), first), pl.BlockSpec((k, n), second)]
            + [out] * (more is not None),
            out_specs=out,
        ),
        out_shape=jax.ShapeDtypeStruct((m, n), bf16),
        compiler_params=pltpu.CompilerParams(
            dimension_semantics=("arbitrary",), vmem_limit_bytes=24 * 1024 * 1024
        ),
        cost_estimate=pl.CostEstimate(flops=1, bytes_accessed=1, transcendentals=0),
    )(half, *args)


def stack_heads(a, heads):
    w = a.shape[1] // heads
    return jnp.concatenate([a[:, h * w : (h + 1) * w] for h in range(heads)], axis=0)


def attend_forward(
    bounds, q_ref, k_ref, v_ref, low_ref, pos_ref, o_ref, lse_ref, *, heads, span, scale
):
    chunk = pl.program_id(0)
    rows = stack_heads(q_ref[...], heads)
    n, width = rows.shape
    low = jnp.concatenate([low_ref[0]] * heads, axis=1)
    pos = jnp.concatenate([pos_ref[0]] * heads, axis=1)

    def step(kb, state):
        top, total, acc = state
        start = pl.multiple_of(kb * span, span)
        keys = k_ref[pl.ds(start, span), :]
        values = v_ref[pl.ds(start, span), :]
        s = dot_nt(keys, rows) * scale
        at = start + lax.broadcasted_iota(jnp.int32, (span, n), 0)
        s = jnp.where((at >= low) & (at <= pos), s, negative)
        new = jnp.maximum(top, jnp.max(s, axis=0, keepdims=True))
        p = jnp.exp2(s - new)
        fade = jnp.exp2(top - new)
        total = total * fade + jnp.sum(p, axis=0, keepdims=True)
        acc = acc * fade + dot_tn(values, p.astype(bf16))
        return new, total, acc

    start_state = (
        jnp.full((1, n), negative, f32),
        jnp.zeros((1, n), f32),
        jnp.zeros((width, n), f32),
    )
    top, total, acc = lax.fori_loop(bounds[chunk, 0], bounds[chunk, 1], step, start_state)
    out = (acc / total).T.astype(bf16)
    t = n // heads
    for h in range(heads):
        o_ref[:, h * width : (h + 1) * width] = out[h * t : (h + 1) * t]
    lse_ref[0] = top + jnp.log2(total)


def attend_backward(
    bounds, q_ref, o_ref, g_ref, lse_ref, k_ref, v_ref, low_ref, pos_ref, dq_ref, dkv_ref, *, heads, span, scale, plain
):
    chunk = pl.program_id(0)

    @pl.when(chunk == 0)
    def _():
        dkv_ref[...] = jnp.zeros_like(dkv_ref)

    rows = stack_heads(q_ref[...], heads)
    outs = stack_heads(o_ref[...], heads)
    grads = stack_heads(g_ref[...], heads)
    n, width = rows.shape
    low = jnp.concatenate([low_ref[0]] * heads, axis=1)
    pos = jnp.concatenate([pos_ref[0]] * heads, axis=1)
    lse = lse_ref[0]
    delta = jnp.sum((outs.astype(f32) * grads.astype(f32)).T, axis=0, keepdims=True)

    def step(kb, acc):
        start = pl.multiple_of(kb * span, span)
        keys = k_ref[pl.ds(start, span), :]
        values = v_ref[pl.ds(start, span), :]
        s = dot_nt(keys, rows) * scale
        at = start + lax.broadcasted_iota(jnp.int32, (span, n), 0)
        p = jnp.where((at >= low) & (at <= pos), jnp.exp2(s - lse), 0.0)
        dp = dot_nt(values, grads)
        ds = (p * (dp - delta)).astype(bf16)
        acc = acc + dot_tn(keys, ds)
        dkv_ref[pl.ds(start, span), :width] += dot_nn(ds, rows) * plain
        dkv_ref[pl.ds(start, span), width:] += dot_nn(p.astype(bf16), grads)
        return acc

    acc = lax.fori_loop(bounds[chunk, 0], bounds[chunk, 1], step, jnp.zeros((width, n), f32))
    out = (acc * plain).T.astype(bf16)
    t = n // heads
    for h in range(heads):
        dq_ref[:, h * width : (h + 1) * width] = out[h * t : (h + 1) * t]


class Attention:
    def __init__(self, tokens, chunks, hidden, length, head):
        self.t, self.chunks, self.hidden, self.length, self.head = tokens, chunks, hidden, length, head
        self.heads = hidden // head
        self.span = min(512, length)
        self.plain = head ** (-0.5)
        self.scale = self.plain * log2e
        self.params = pltpu.CompilerParams(
            dimension_semantics=("arbitrary",), vmem_limit_bytes=(20 << 20) + length * 4096
        )
        self.rows_spec = pl.BlockSpec((tokens, hidden), lambda i, b: (i, 0))
        self.kv_spec = pl.BlockSpec((length, head), lambda i, b: (0, 0))
        self.vec_spec = pl.BlockSpec((1, 1, tokens), lambda i, b: (i, 0, 0))
        self.lse_spec = pl.BlockSpec((1, 1, tokens * self.heads), lambda i, b: (i, 0, 0))
        self.cells = tokens * chunks * self.heads * length

    def forward(self, bounds, q, k, v, low, pos):
        body = functools.partial(attend_forward, heads=self.heads, span=self.span, scale=self.scale)
        return pl.pallas_call(
            body,
            grid_spec=pltpu.PrefetchScalarGridSpec(
                num_scalar_prefetch=1,
                grid=(self.chunks,),
                in_specs=[self.rows_spec, self.kv_spec, self.kv_spec, self.vec_spec, self.vec_spec],
                out_specs=[self.rows_spec, self.lse_spec],
            ),
            out_shape=[
                jax.ShapeDtypeStruct(q.shape, bf16),
                jax.ShapeDtypeStruct((self.chunks, 1, self.t * self.heads), f32),
            ],
            compiler_params=self.params,
            cost_estimate=pl.CostEstimate(
                flops=4 * self.cells * self.head, bytes_accessed=4 << 20, transcendentals=self.cells
            ),
        )(bounds, q, k, v, low, pos)

    def backward(self, bounds, q, o, g, lse, k, v, low, pos):
        body = functools.partial(
            attend_backward, heads=self.heads, span=self.span, scale=self.scale, plain=self.plain
        )
        return pl.pallas_call(
            body,
            grid_spec=pltpu.PrefetchScalarGridSpec(
                num_scalar_prefetch=1,
                grid=(self.chunks,),
                in_specs=[self.rows_spec] * 3
                + [self.lse_spec, self.kv_spec, self.kv_spec, self.vec_spec, self.vec_spec],
                out_specs=[
                    self.rows_spec,
                    pl.BlockSpec((self.length, 2 * self.head), lambda i, b: (0, 0)),
                ],
            ),
            out_shape=[
                jax.ShapeDtypeStruct(q.shape, bf16),
                jax.ShapeDtypeStruct((self.length, 2 * self.head), f32),
            ],
            compiler_params=self.params,
            cost_estimate=pl.CostEstimate(
                flops=10 * self.cells * self.head, bytes_accessed=8 << 20, transcendentals=self.cells
            ),
        )(bounds, q, o, g, lse, k, v, low, pos)


def norm_parts(v):
    mean = jnp.mean(v, axis=1, keepdims=True)
    spread = jnp.mean(v * v, axis=1, keepdims=True) - mean * mean
    inv_std = lax.rsqrt(spread + epsilon)
    return (v - mean) * inv_std, inv_std


def norm_back(part, near, far, base, centred, inv_std, gain, kv=None, weight=None):
    t, width = near.shape
    more = () if kv is None else (kv, weight)

    def body(p_ref, n_ref, f_ref, b_ref, c_ref, i_ref, g_ref, *refs):
        e = p_ref[...].astype(f32) + n_ref[...].astype(f32) + f_ref[...].astype(f32)
        if more:
            e = e + dot_nt(refs[0][...], refs[1][...])
        grad_ref, low_ref, sum_ref = refs[-3:]
        centre = c_ref[...]
        c = e * g_ref[...]
        m1 = jnp.sum(c, axis=1, keepdims=True) * (1.0 / width)
        m2 = jnp.sum(c * centre, axis=1, keepdims=True) * (1.0 / width)
        grad = b_ref[...].astype(f32) + (c - m1 - centre * m2) * i_ref[...]
        low = grad.astype(bf16)
        grad_ref[...] = grad
        low_ref[...] = low
        total = lambda a: jnp.sum(a, axis=0, keepdims=True)
        sums = [total(e * centre), total(e), total(low.astype(f32)), jnp.zeros((5, width), f32)]
        sum_ref[...] = jnp.concatenate(sums, axis=0)

    whole = lambda a: pl.BlockSpec(a.shape, lambda i: (0, 0))
    args = (part, near, far, base, centred, inv_std, gain, *more)
    shapes = [
        jax.ShapeDtypeStruct((t, width), f32),
        jax.ShapeDtypeStruct((t, width), bf16),
        jax.ShapeDtypeStruct((8, width), f32),
    ]
    return pl.pallas_call(
        body,
        grid=(1,),
        in_specs=[pl.BlockSpec((t, width), lambda i: (0, 0))] + [whole(a) for a in args[1:]],
        out_specs=[whole(a) for a in shapes],
        out_shape=shapes,
        compiler_params=pltpu.CompilerParams(
            dimension_semantics=("arbitrary",), vmem_limit_bytes=32 * 1024 * 1024
        ),
        cost_estimate=pl.CostEstimate(flops=20 * t * width, bytes_accessed=20 * t * width, transcendentals=0),
    )(*args)


gelu_a = math.sqrt(2.0 / math.pi)
gelu_b = 0.044715


def per_device(
    tokens,
    segment_ids,
    ln1_gain,
    ln1_bias,
    w_query,
    b_query,
    w_keyval,
    b_value,
    w_out,
    b_out,
    ln2_gain,
    ln2_bias,
    w_up,
    b_up,
    w_down,
    b_down,
    d_output,
):
    at = Place()
    rows = at.rows
    col_tokens, row_width = tokens.shape
    t = col_tokens // rows
    width = row_width * rows
    head = b_value.shape[0]
    hidden = w_query.shape[1]
    length = segment_ids.shape[1]
    row, col = at.ry * 2 + at.rx, at.ch * 2 + at.cl
    every = ("ry", "rx", "dp")
    rows_of = lambda a, n: lambda r: lax.dynamic_slice_in_dim(a, r * n, n, 0)
    lanes_of = lambda a, n: lambda r: lax.dynamic_slice_in_dim(a, r * n, n, 1)

    gather = lambda w, axis: lax.all_gather(half_of(w, axis), every, axis=axis, tiled=True)
    qkvo_weight = gather(jnp.concatenate([w_query, w_keyval, w_out.T], axis=1), 0)
    qkv_weight, out_weight = qkvo_weight[:, : hidden + 2 * head], qkvo_weight[:, hidden + 2 * head :]
    down_weight = gather(w_down, 1)
    up_weight = gather(w_up, 0)

    vectors = jnp.pad(jnp.stack([ln1_gain, ln1_bias, ln2_gain, ln2_bias, b_out, b_down]), ((0, 10), (0, 0)))
    got = at.exchange(rows_of(tokens, t), lambda r: vectors)
    got = at.by_lanes(got, 0, got[0].shape[0])
    got, d_output = tie(got, d_output)
    own = got[:t].astype(f32)
    gain_one, bias_one, gain_two, bias_two, out_bias, down_bias = got[t : t + 6].astype(f32)[:, None, :]
    own_grad = at.to_tokens(d_output)

    segments = segment_ids[0]
    base = jnp.stack([(col ^ k) * col_tokens + row * t for k in range(4)]).astype(jnp.int32)
    pos = base[:, None] + jnp.arange(t, dtype=jnp.int32)[None, :]
    seg_rows = jnp.stack([lax.dynamic_slice_in_dim(segments, base[k], t, 0) for k in range(4)])
    low = jnp.sum((segments[None, None, :] < seg_rows[:, :, None]).astype(jnp.int32), axis=2)
    attention = Attention(t, 4, hidden, length, head)
    span = attention.span
    bounds = jnp.stack([low[:, 0] // span, (base + t - 1) // span + 1], axis=1)
    low, pos = low[:, None, :], pos[:, None, :]

    centred_one, inv_one = norm_parts(own)
    normed_one = (centred_one * gain_one + bias_one).astype(bf16)
    block_one = line_second(normed_one, *tie(*line_first(normed_one)))
    block_one, own_grad = tie(block_one, own_grad)
    kv_bias = jnp.pad(b_value.astype(f32), (head, 0))
    kv = (dot_nn(block_one, qkv_weight[:, hidden:]) + kv_bias).astype(bf16)
    got = at.exchange(lambda r: kv)
    queries = (dot_nn(block_one, qkv_weight[:, :hidden]) + b_query.astype(f32)).astype(bf16)
    grad_first = line_first(own_grad)
    kv = at.by_tokens(got, col, t)
    keys, values = kv[:, :head], kv[:, head:]
    attended, lse = attention.forward(bounds, queries, keys, values, low, pos)

    part = dot_nt(attended, out_weight).astype(bf16)
    part, grad_first = tie(part, grad_first)
    block_grad = line_second(own_grad, *grad_first)
    end, near = line_scatter_first(part)
    far = line_scatter_second(part, end)
    near, far, block_grad = tie(near, far, block_grad)
    hidden_one = own + out_bias + line_total(part, near, far)
    centred_two, inv_two = norm_parts(hidden_one)
    normed_two = (centred_two * gain_two + bias_two).astype(bf16)
    far, near = line_first(normed_two)
    grad_act = multiply(block_grad, down_weight, "nt")
    far, near, grad_act = tie(far, near, grad_act)
    block_two = line_second(normed_two, far, near)

    core = at.dp.astype(jnp.int32).reshape(1)
    activated, grad_upper = feed_forward(block_two, up_weight, b_up.astype(f32)[None, :], grad_act)
    part = multiply(grad_upper, up_weight, "nt")
    part, activated, grad_upper = tie(part, activated, grad_upper)
    end, near = line_scatter_first(part)
    down_part = outer(1 - core, activated, block_grad, 0)
    up_part = outer(1 - core, block_two, grad_upper, 1)
    end, down_part, up_part, activated, grad_upper = tie(end, down_part, up_part, activated, grad_upper)
    far = line_scatter_second(part, end)
    down_part, up_part = swap(down_part, "dp"), swap(up_part, "dp")
    down_part = outer(core, activated, block_grad, 0, down_part)
    up_part = outer(core, block_two, grad_upper, 1, up_part)
    near, far, down_part, up_part, activated = tie(near, far, down_part, up_part, activated)
    down_part = scatter_row(down_part, 1)
    up_part = scatter_row(up_part, 0)
    grad_hidden, grad_branch, sums_two = norm_back(
        part, near, far, own_grad, centred_two, inv_two, gain_two
    )
    far, near = line_first(grad_branch)
    far, near, activated = tie(far, near, activated)
    block_branch = line_second(grad_branch, far, near)
    grad_att = dot_nn(block_branch, out_weight).astype(bf16)
    grad_query, grad_kv = attention.backward(
        bounds, queries, attended, grad_att, lse, keys, values, low, pos
    )

    grad_kv = grad_kv.astype(bf16)
    grad_query, grad_kv, block_branch, attended, activated = tie(
        grad_query, grad_kv, block_branch, attended, activated
    )
    final_part = multiply(activated, down_weight, "nn", 1)
    part = dot_nt(grad_query, qkv_weight[:, :hidden]).astype(bf16)
    end, near = line_scatter_first(part)
    kv_grad = at.sum_rows(lambda r: at.line_tokens(grad_kv, col, r, t)).astype(bf16)
    far = line_scatter_second(part, end)
    kv_grad, grad_query, block_one, down_part = tie(kv_grad, grad_query, block_one, down_part)
    parts = [dot_tn(block_one, grad_query).astype(bf16), dot_tn(block_branch, attended).astype(bf16)]
    qo_part = jnp.concatenate(parts, axis=1)
    cut = lambda k: kv_grad[k * t : (k + 1) * t]
    got = swap(jnp.concatenate([cut(1), cut(3)], axis=0), "cl")
    got, final_part, qo_part = tie(got, final_part, qo_part)
    kv_own = add(add(cut(0), got[:t]), swap(add(cut(2), got[t:]), "ch"))
    final_end, final_near = line_scatter_first(final_part)
    near, far, kv_own, up_part = tie(near, far, kv_own, up_part)
    qo_part = lax.psum_scatter(qo_part, ("ry", "rx", "dp"), scatter_dimension=0, tiled=True)
    unused, grad_own, sums_one = norm_back(
        part, near, far, grad_hidden, centred_one, inv_one, gain_one, kv_own, qkv_weight[:, hidden : hidden + 2 * head]
    )

    kv_part = dot_tn(kv_own, normed_one).astype(bf16)
    kv_far = swap(lax.dynamic_slice_in_dim(kv_part, (1 - at.dp) * head, head, 0), "dp")
    kv_part = add(half_of(kv_part, 0), kv_far)

    sums = lambda a: jnp.sum(a.astype(f32), axis=0)
    tiled = lambda a: jnp.tile(a.reshape(-1, row_width), (1, rows))
    place = lambda a: lax.dynamic_update_slice_in_dim(jnp.zeros((4 * a.shape[0],), f32), a, col * a.shape[0], 0)
    parts = [
        sums_two[:3],
        sums(own_grad)[None],
        tiled(jnp.pad(sums(kv_own[:, head:]), (0, row_width - head))),
        tiled(place(sums(grad_query))),
        tiled(place(sums(grad_upper))),
    ]
    n = sum(p.shape[0] for p in parts)
    parts.append(jnp.zeros((-n % 16, width), f32))
    packed = jnp.concatenate(parts).astype(bf16)
    n = packed.shape[0]
    late = jnp.pad(sums_one, ((0, 8), (0, 0))).astype(bf16)
    grad_own, final_end, down_part = tie(grad_own, final_end, down_part)
    final_far = line_scatter_second(final_part, final_end)
    grad_w_down = at.both_cores(down_part, 0)
    got = at.exchange(*(lanes_of(a, row_width) for a in (packed, late, kv_part, grad_own)))
    n = n + 16
    total = sum(g[: n + head].astype(f32) for g in got)
    grad_tokens = at.by_rows(got, n + head, n + head + t).astype(f32)
    total, final_near, final_far = tie(total, final_near, final_far)
    final = hidden_one + down_bias + line_total(final_part, final_near, final_far)
    output = at.by_rows(at.exchange(lanes_of(final.astype(bf16), row_width)), 0, t)
    total = total.astype(bf16)
    both = lax.ppermute(total, ("ch", "cl"), [(0, 3), (3, 0), (1, 2), (2, 1)])
    sides = [total, swap(total, "ch"), swap(total, "cl"), both]
    lower = (sides[0].astype(f32) + sides[1].astype(f32)) + (sides[2].astype(f32) + sides[3].astype(f32))
    total = lower
    total = gather_axis(total.astype(bf16), "dp").astype(f32)
    grad_w_keyval = total[:, n:].reshape(2 * head, row_width).T
    total = total[0, :n] + total[1, :n]
    qo_part = at.both_cores(qo_part, 0)
    grad_w_query, grad_w_out = qo_part[:, :hidden], qo_part[:, hidden:].T
    grad_w_up = at.both_cores(up_part, 1)
    grad_ln2_gain, grad_ln2_bias, grad_b_out, grad_b_down = total[:4]
    grad_ln1_gain, grad_ln1_bias = total[n - 16], total[n - 15]
    grad_b_value = total[4, :head]
    of_col = lambda first, n: lax.dynamic_slice_in_dim(
        total[first : first + 4 * n // row_width].reshape(-1), col * n, n, 0
    )
    grad_b_query = of_col(5, hidden)
    grad_b_up = of_col(5 + 4 * hidden // row_width, b_up.shape[0])
    return (
        output,
        grad_tokens,
        grad_ln1_gain,
        grad_ln1_bias,
        grad_w_query,
        grad_b_query,
        grad_w_keyval,
        grad_b_value,
        grad_w_out,
        grad_b_out,
        grad_ln2_gain,
        grad_ln2_bias,
        grad_w_up,
        grad_b_up,
        grad_w_down,
        grad_b_down,
    )


def solution(mesh):
    dp, rows, cols = (mesh.shape[name] for name in ("dp", "row", "col"))
    fine = Mesh(
        mesh.devices.reshape(dp, rows // 2, 2, cols // 2, 2), ("dp", "ry", "rx", "ch", "cl")
    )
    row, col = ("ry", "rx"), ("ch", "cl")
    tok = P(("dp", "ch", "cl"), row)
    in_specs = (
        tok,
        P("dp", None),
        P(row),
        P(row),
        P(row, col),
        P(col),
        P(row, None),
        P(),
        P(col, row),
        P(row),
        P(row),
        P(row),
        P(row, col),
        P(col),
        P(col, row),
        P(row),
        tok,
    )
    out_specs = (
        tok,
        tok,
        P(row),
        P(row),
        P(row, col),
        P(col),
        P(row, None),
        P(),
        P(col, row),
        P(row),
        P(row),
        P(row),
        P(row, col),
        P(col),
        P(col, row),
        P(row),
    )
    return jax.shard_map(
        per_device, mesh=fine, in_specs=in_specs, out_specs=out_specs, check_vma=False
    )
```

```python
import functools
import math

import jax
import jax.numpy as jnp
from jax import lax
from jax.experimental import pallas as pl
from jax.experimental.pallas import tpu as pltpu
from jax.sharding import Mesh
from jax.sharding import PartitionSpec as P

epsilon = 1e-05
negative = -1e30
log2e = math.log2(math.e)
f32 = jnp.float32
bf16 = jnp.bfloat16


def dot_nn(a, b):
    return lax.dot_general(a, b, (((1,), (0,)), ((), ())), preferred_element_type=f32)


def dot_nt(a, b):
    return lax.dot_general(a, b, (((1,), (1,)), ((), ())), preferred_element_type=f32)


def dot_tn(a, b):
    return lax.dot_general(a, b, (((0,), (0,)), ((), ())), preferred_element_type=f32)


def swap(a, axis):
    return lax.ppermute(a, axis, [(0, 1), (1, 0)])


def fetch(a, axis, step):
    n = lax.axis_size(axis)
    return lax.ppermute(a, axis, [(s, (s - step) % n) for s in range(n)])


def tie(*arrays):
    return jax.tree.unflatten(
        jax.tree.structure(arrays), lax.optimization_barrier(tuple(jax.tree.leaves(arrays)))
    )


def add(u, v):
    return (u.astype(f32) + v.astype(f32)).astype(bf16)


def line_first(a):
    return swap(a, "ch"), swap(a, "cl")


def line_second(a, far, near):
    return jnp.concatenate([a, near, far, swap(far, "cl")], axis=0)


def line_scatter_first(p):
    t = p.shape[0] // 4
    return swap(p[3 * t :], "cl"), swap(p[t : 2 * t], "cl")


def line_scatter_second(p, end):
    t = p.shape[0] // 4
    return swap(add(p[2 * t : 3 * t], end), "ch")


def line_total(p, near, far):
    return p[: near.shape[0]].astype(f32) + near.astype(f32) + far.astype(f32)


def gather_axis(a, axis):
    n = lax.axis_size(axis)
    if n == 2:
        b = swap(a, axis)
        first = lax.axis_index(axis) == 0
        return jnp.stack([jnp.where(first, a, b), jnp.where(first, b, a)])
    return lax.all_gather(a, axis, axis=0, tiled=False)


def row_send(a, k, rows):
    n, j, i = rows // 2, k // 2, k % 2
    pairs = [(y * 2 + x, (y + j) % n * 2 + (x ^ i)) for y in range(n) for x in range(2)]
    return lax.ppermute(a, ("ry", "rx"), pairs)


def half_of(w, axis):
    n = w.shape[axis] // 2
    return lax.dynamic_slice_in_dim(w, lax.axis_index("dp") * n, n, axis)


def scatter_row(g, feat):
    return lax.psum_scatter(g, ("ry", "rx"), scatter_dimension=feat, tiled=True)


class Place:
    def __init__(self):
        self.dp = lax.axis_index("dp")
        self.ry = lax.axis_index("ry")
        self.rx = lax.axis_index("rx")
        self.ch = lax.axis_index("ch")
        self.cl = lax.axis_index("cl")
        self.rows_y = lax.axis_size("ry")
        self.rows = 2 * self.rows_y

    def row_of(self, k):
        return ((self.ry + k // 2) % self.rows_y) * 2 + (self.rx ^ (k % 2))

    def row_from(self, k):
        return ((self.ry - k // 2) % self.rows_y) * 2 + (self.rx ^ (k % 2))

    def slot_from(self, r):
        return ((self.ry - r // 2) % self.rows_y) * 2 + (self.rx ^ (r % 2))

    def both_cores(self, part, feat):
        pair = gather_axis(part, "dp")
        return jnp.concatenate([pair[0], pair[1]], axis=feat).astype(f32)

    def by_tokens(self, got, col, t):
        got = jnp.concatenate(got, axis=0)
        at = lambda c, r: (self.slot_from(r) * 4 + (col ^ c)) * t
        return jnp.concatenate(
            [lax.dynamic_slice_in_dim(got, at(c, r), t, 0) for c in range(4) for r in range(self.rows)], axis=0
        )

    def sum_rows(self, lines):
        pair = lambda y: jnp.concatenate([lines(2 * y), lines(2 * y + 1)], axis=0)
        total = pair(self.ry).astype(f32)
        for j in range(1, self.rows_y):
            total = total + row_send(pair((self.ry + j) % self.rows_y), 2 * j, self.rows).astype(f32)
        n = total.shape[0] // 2
        cut = lambda x: lax.dynamic_slice_in_dim(total, x * n, n, 0)
        return cut(self.rx) + swap(cut(1 - self.rx).astype(bf16), "rx").astype(f32)

    def line_tokens(self, a, col, r, t):
        return jnp.concatenate(
            [lax.dynamic_slice_in_dim(a, ((col ^ k) * self.rows + r) * t, t, 0) for k in range(4)], axis=0
        )

    def exchange(self, *parts):
        got = []
        for k in range(self.rows):
            r = self.row_of(k)
            part = jnp.concatenate([p(r) for p in parts], axis=0) if len(parts) > 1 else parts[0](r)
            got.append(row_send(part, k, self.rows) if k else part)
        return got

    def to_tokens(self, a):
        n, w = a.shape[0] // self.rows, a.shape[1]
        cut = lambda y: lax.dynamic_slice_in_dim(a, y * 2 * n, 2 * n, 0)
        got = [cut(self.ry)]
        got += [row_send(cut((self.ry + j) % self.rows_y), 2 * j, self.rows) for j in range(1, self.rows_y)]
        got = jnp.concatenate(got, axis=1)
        part = lambda x: lax.dynamic_slice_in_dim(got, x * n, n, 0)
        got = jnp.concatenate([part(self.rx), swap(part(1 - self.rx), "rx")], axis=1)
        slot = lambda r: ((r % 2) ^ self.rx) * self.rows_y + (self.ry - r // 2) % self.rows_y
        return jnp.concatenate(
            [lax.dynamic_slice_in_dim(got, slot(r) * w, w, 1) for r in range(self.rows)], axis=1
        )

    def by_lanes(self, got, lo, hi):
        w = got[0].shape[1]
        got = jnp.concatenate([g[lo:hi] for g in got], axis=1)
        return jnp.concatenate(
            [lax.dynamic_slice_in_dim(got, self.slot_from(r) * w, w, 1) for r in range(self.rows)], axis=1
        )

    def by_rows(self, got, lo, hi):
        n = hi - lo
        got = jnp.concatenate([g[lo:hi] for g in got], axis=0)
        return jnp.concatenate(
            [lax.dynamic_slice_in_dim(got, self.slot_from(r) * n, n, 0) for r in range(self.rows)], axis=0
        )


def multiply(x, w, kind, cost=None):
    def body(x_ref, w_ref, o_ref):
        dot = {"nn": dot_nn, "nt": dot_nt, "tn": dot_tn}[kind]
        o_ref[...] = dot(x_ref[...], w_ref[...]).astype(bf16)

    whole = lambda a: pl.BlockSpec(a.shape, lambda i: (0, 0))
    if kind == "tn":
        m, n, k = x.shape[1], w.shape[1], x.shape[0]
        tile = min(512, m)
        specs = [pl.BlockSpec((k, tile), lambda i: (0, i)), whole(w)]
        out_spec, steps = pl.BlockSpec((tile, n), lambda i: (i, 0)), m // tile
    else:
        m, k = x.shape
        n = w.shape[1] if kind == "nn" else w.shape[0]
        tile = min(512, n)
        by_col, by_row = pl.BlockSpec((k, tile), lambda i: (0, i)), pl.BlockSpec((tile, k), lambda i: (i, 0))
        specs = [whole(x), by_col if kind == "nn" else by_row]
        out_spec, steps = pl.BlockSpec((m, tile), lambda i: (0, i)), n // tile
    return pl.pallas_call(
        body,
        grid=(steps,),
        in_specs=specs,
        out_specs=out_spec,
        out_shape=jax.ShapeDtypeStruct((m, n), bf16),
        compiler_params=pltpu.CompilerParams(
            dimension_semantics=("arbitrary",), vmem_limit_bytes=24 * 1024 * 1024
        ),
        cost_estimate=pl.CostEstimate(
            flops=2 * m * n * k if cost is None else cost,
            bytes_accessed=2 * (m * n + m * k + n * k) if cost is None else cost,
            transcendentals=0,
        ),
    )(x, w)


def feed_forward(x, w, bias, grad_act):
    (m, k), n = x.shape, w.shape[1]
    tile = min(512, n)

    def body(x_ref, w_ref, b_ref, g_ref, a_ref, u_ref):
        u = dot_nn(x_ref[...], w_ref[...]) + b_ref[...]
        square = u * u
        th = jnp.tanh(gelu_a * u * (1.0 + gelu_b * square))
        half = 0.5 * (1.0 + th)
        a_ref[...] = (u * half).astype(bf16)
        slope = half + 0.5 * u * (1.0 - th * th) * (gelu_a + 3.0 * gelu_a * gelu_b * square)
        u_ref[...] = (g_ref[...].astype(f32) * slope).astype(bf16)

    cols = lambda rows: pl.BlockSpec((rows, tile), lambda i: (0, i))
    return pl.pallas_call(
        body,
        grid=(n // tile,),
        in_specs=[pl.BlockSpec((m, k), lambda i: (0, 0)), cols(k), cols(1), cols(m)],
        out_specs=[cols(m), cols(m)],
        out_shape=[jax.ShapeDtypeStruct((m, n), bf16)] * 2,
        compiler_params=pltpu.CompilerParams(
            dimension_semantics=("arbitrary",), vmem_limit_bytes=24 * 1024 * 1024
        ),
        cost_estimate=pl.CostEstimate(
            flops=2 * m * n * k, bytes_accessed=2 * (3 * m * n + m * k + n * k), transcendentals=m * n
        ),
    )(x, w, bias, grad_act)


def outer(half, x, y, split, more=None):
    k, m, n = x.shape[0], x.shape[1], y.shape[1]
    m, n = (m // 2, n) if split == 0 else (m, n // 2)
    tile = min(512, m)
    steps = m // tile

    def body(half_ref, x_ref, y_ref, *refs):
        total = dot_tn(x_ref[...], y_ref[...])
        if more is not None:
            total = total + refs[0][...].astype(f32)
        refs[-1][...] = total.astype(bf16)

    out = pl.BlockSpec((tile, n), lambda i, half: (i, 0))
    first = (lambda i, half: (0, half[0] * steps + i)) if split == 0 else (lambda i, half: (0, i))
    second = (lambda i, half: (0, 0)) if split == 0 else (lambda i, half: (0, half[0]))
    args = (x, y) if more is None else (x, y, more)
    return pl.pallas_call(
        body,
        grid_spec=pltpu.PrefetchScalarGridSpec(
            num_scalar_prefetch=1,
            grid=(steps,),
            in_specs=[pl.BlockSpec((k, tile), first), pl.BlockSpec((k, n), second)]
            + [out] * (more is not None),
            out_specs=out,
        ),
        out_shape=jax.ShapeDtypeStruct((m, n), bf16),
        compiler_params=pltpu.CompilerParams(
            dimension_semantics=("arbitrary",), vmem_limit_bytes=24 * 1024 * 1024
        ),
        cost_estimate=pl.CostEstimate(flops=1, bytes_accessed=1, transcendentals=0),
    )(half, *args)


def stack_heads(a, heads):
    w = a.shape[1] // heads
    return jnp.concatenate([a[:, h * w : (h + 1) * w] for h in range(heads)], axis=0)


def attend_forward(
    bounds, q_ref, k_ref, v_ref, low_ref, pos_ref, o_ref, lse_ref, *, heads, span, scale
):
    chunk = pl.program_id(0)
    rows = stack_heads(q_ref[...], heads)
    n, width = rows.shape
    low = jnp.concatenate([low_ref[0]] * heads, axis=1)
    pos = jnp.concatenate([pos_ref[0]] * heads, axis=1)

    def step(kb, state):
        top, total, acc = state
        start = pl.multiple_of(kb * span, span)
        keys = k_ref[pl.ds(start, span), :]
        values = v_ref[pl.ds(start, span), :]
        s = dot_nt(keys, rows) * scale
        at = start + lax.broadcasted_iota(jnp.int32, (span, n), 0)
        s = jnp.where((at >= low) & (at <= pos), s, negative)
        new = jnp.maximum(top, jnp.max(s, axis=0, keepdims=True))
        p = jnp.exp2(s - new)
        fade = jnp.exp2(top - new)
        total = total * fade + jnp.sum(p, axis=0, keepdims=True)
        acc = acc * fade + dot_tn(values, p.astype(bf16))
        return new, total, acc

    start_state = (
        jnp.full((1, n), negative, f32),
        jnp.zeros((1, n), f32),
        jnp.zeros((width, n), f32),
    )
    top, total, acc = lax.fori_loop(bounds[chunk, 0], bounds[chunk, 1], step, start_state)
    out = (acc / total).T.astype(bf16)
    t = n // heads
    for h in range(heads):
        o_ref[:, h * width : (h + 1) * width] = out[h * t : (h + 1) * t]
    lse_ref[0] = top + jnp.log2(total)


def attend_backward(
    bounds, q_ref, o_ref, g_ref, lse_ref, k_ref, v_ref, low_ref, pos_ref, dq_ref, dkv_ref, *, heads, span, scale, plain
):
    chunk = pl.program_id(0)

    @pl.when(chunk == 0)
    def _():
        dkv_ref[...] = jnp.zeros_like(dkv_ref)

    rows = stack_heads(q_ref[...], heads)
    outs = stack_heads(o_ref[...], heads)
    grads = stack_heads(g_ref[...], heads)
    n, width = rows.shape
    low = jnp.concatenate([low_ref[0]] * heads, axis=1)
    pos = jnp.concatenate([pos_ref[0]] * heads, axis=1)
    lse = lse_ref[0]
    delta = jnp.sum((outs.astype(f32) * grads.astype(f32)).T, axis=0, keepdims=True)

    def step(kb, acc):
        start = pl.multiple_of(kb * span, span)
        keys = k_ref[pl.ds(start, span), :]
        values = v_ref[pl.ds(start, span), :]
        s = dot_nt(keys, rows) * scale
        at = start + lax.broadcasted_iota(jnp.int32, (span, n), 0)
        p = jnp.where((at >= low) & (at <= pos), jnp.exp2(s - lse), 0.0)
        dp = dot_nt(values, grads)
        ds = (p * (dp - delta)).astype(bf16)
        acc = acc + dot_tn(keys, ds)
        dkv_ref[pl.ds(start, span), :width] += dot_nn(ds, rows) * plain
        dkv_ref[pl.ds(start, span), width:] += dot_nn(p.astype(bf16), grads)
        return acc

    acc = lax.fori_loop(bounds[chunk, 0], bounds[chunk, 1], step, jnp.zeros((width, n), f32))
    out = (acc * plain).T.astype(bf16)
    t = n // heads
    for h in range(heads):
        dq_ref[:, h * width : (h + 1) * width] = out[h * t : (h + 1) * t]


class Attention:
    def __init__(self, tokens, chunks, hidden, length, head):
        self.t, self.chunks, self.hidden, self.length, self.head = tokens, chunks, hidden, length, head
        self.heads = hidden // head
        self.span = min(512, length)
        self.plain = head ** (-0.5)
        self.scale = self.plain * log2e
        self.params = pltpu.CompilerParams(
            dimension_semantics=("arbitrary",), vmem_limit_bytes=(20 << 20) + length * 4096
        )
        self.rows_spec = pl.BlockSpec((tokens, hidden), lambda i, b: (i, 0))
        self.kv_spec = pl.BlockSpec((length, head), lambda i, b: (0, 0))
        self.vec_spec = pl.BlockSpec((1, 1, tokens), lambda i, b: (i, 0, 0))
        self.lse_spec = pl.BlockSpec((1, 1, tokens * self.heads), lambda i, b: (i, 0, 0))
        self.cells = tokens * chunks * self.heads * length

    def forward(self, bounds, q, k, v, low, pos):
        body = functools.partial(attend_forward, heads=self.heads, span=self.span, scale=self.scale)
        return pl.pallas_call(
            body,
            grid_spec=pltpu.PrefetchScalarGridSpec(
                num_scalar_prefetch=1,
                grid=(self.chunks,),
                in_specs=[self.rows_spec, self.kv_spec, self.kv_spec, self.vec_spec, self.vec_spec],
                out_specs=[self.rows_spec, self.lse_spec],
            ),
            out_shape=[
                jax.ShapeDtypeStruct(q.shape, bf16),
                jax.ShapeDtypeStruct((self.chunks, 1, self.t * self.heads), f32),
            ],
            compiler_params=self.params,
            cost_estimate=pl.CostEstimate(
                flops=4 * self.cells * self.head, bytes_accessed=4 << 20, transcendentals=self.cells
            ),
        )(bounds, q, k, v, low, pos)

    def backward(self, bounds, q, o, g, lse, k, v, low, pos):
        body = functools.partial(
            attend_backward, heads=self.heads, span=self.span, scale=self.scale, plain=self.plain
        )
        return pl.pallas_call(
            body,
            grid_spec=pltpu.PrefetchScalarGridSpec(
                num_scalar_prefetch=1,
                grid=(self.chunks,),
                in_specs=[self.rows_spec] * 3
                + [self.lse_spec, self.kv_spec, self.kv_spec, self.vec_spec, self.vec_spec],
                out_specs=[
                    self.rows_spec,
                    pl.BlockSpec((self.length, 2 * self.head), lambda i, b: (0, 0)),
                ],
            ),
            out_shape=[
                jax.ShapeDtypeStruct(q.shape, bf16),
                jax.ShapeDtypeStruct((self.length, 2 * self.head), f32),
            ],
            compiler_params=self.params,
            cost_estimate=pl.CostEstimate(
                flops=10 * self.cells * self.head, bytes_accessed=8 << 20, transcendentals=self.cells
            ),
        )(bounds, q, o, g, lse, k, v, low, pos)


def norm_parts(v):
    mean = jnp.mean(v, axis=1, keepdims=True)
    spread = jnp.mean(v * v, axis=1, keepdims=True) - mean * mean
    inv_std = lax.rsqrt(spread + epsilon)
    return (v - mean) * inv_std, inv_std


def norm_back(part, near, far, base, centred, inv_std, gain, kv=None, weight=None):
    t, width = near.shape
    more = () if kv is None else (kv, weight)

    def body(p_ref, n_ref, f_ref, b_ref, c_ref, i_ref, g_ref, *refs):
        e = p_ref[...].astype(f32) + n_ref[...].astype(f32) + f_ref[...].astype(f32)
        if more:
            e = e + dot_nt(refs[0][...], refs[1][...])
        grad_ref, low_ref, sum_ref = refs[-3:]
        centre = c_ref[...]
        c = e * g_ref[...]
        m1 = jnp.sum(c, axis=1, keepdims=True) * (1.0 / width)
        m2 = jnp.sum(c * centre, axis=1, keepdims=True) * (1.0 / width)
        grad = b_ref[...].astype(f32) + (c - m1 - centre * m2) * i_ref[...]
        low = grad.astype(bf16)
        grad_ref[...] = grad
        low_ref[...] = low
        total = lambda a: jnp.sum(a, axis=0, keepdims=True)
        sums = [total(e * centre), total(e), total(low.astype(f32)), jnp.zeros((5, width), f32)]
        sum_ref[...] = jnp.concatenate(sums, axis=0)

    whole = lambda a: pl.BlockSpec(a.shape, lambda i: (0, 0))
    args = (part, near, far, base, centred, inv_std, gain, *more)
    shapes = [
        jax.ShapeDtypeStruct((t, width), f32),
        jax.ShapeDtypeStruct((t, width), bf16),
        jax.ShapeDtypeStruct((8, width), f32),
    ]
    return pl.pallas_call(
        body,
        grid=(1,),
        in_specs=[pl.BlockSpec((t, width), lambda i: (0, 0))] + [whole(a) for a in args[1:]],
        out_specs=[whole(a) for a in shapes],
        out_shape=shapes,
        compiler_params=pltpu.CompilerParams(
            dimension_semantics=("arbitrary",), vmem_limit_bytes=32 * 1024 * 1024
        ),
        cost_estimate=pl.CostEstimate(flops=20 * t * width, bytes_accessed=20 * t * width, transcendentals=0),
    )(*args)


gelu_a = math.sqrt(2.0 / math.pi)
gelu_b = 0.044715


def per_device(
    tokens,
    segment_ids,
    ln1_gain,
    ln1_bias,
    w_query,
    b_query,
    w_keyval,
    b_value,
    w_out,
    b_out,
    ln2_gain,
    ln2_bias,
    w_up,
    b_up,
    w_down,
    b_down,
    d_output,
):
    at = Place()
    rows = at.rows
    col_tokens, row_width = tokens.shape
    t = col_tokens // rows
    width = row_width * rows
    head = b_value.shape[0]
    hidden = w_query.shape[1]
    length = segment_ids.shape[1]
    row, col = at.ry * 2 + at.rx, at.ch * 2 + at.cl
    every = ("ry", "rx", "dp")
    rows_of = lambda a, n: lambda r: lax.dynamic_slice_in_dim(a, r * n, n, 0)
    lanes_of = lambda a, n: lambda r: lax.dynamic_slice_in_dim(a, r * n, n, 1)

    gather = lambda w, axis: lax.all_gather(half_of(w, axis), every, axis=axis, tiled=True)
    qkvo_weight = gather(jnp.concatenate([w_query, w_keyval, w_out.T], axis=1), 0)
    qkv_weight, out_weight = qkvo_weight[:, : hidden + 2 * head], qkvo_weight[:, hidden + 2 * head :]
    down_weight = gather(w_down, 1)
    up_weight = gather(w_up, 0)

    vectors = jnp.pad(jnp.stack([ln1_gain, ln1_bias, ln2_gain, ln2_bias, b_out, b_down]), ((0, 10), (0, 0)))
    got = at.exchange(rows_of(tokens, t), lambda r: vectors)
    got = at.by_lanes(got, 0, got[0].shape[0])
    got, d_output = tie(got, d_output)
    own = got[:t].astype(f32)
    gain_one, bias_one, gain_two, bias_two, out_bias, down_bias = got[t : t + 6].astype(f32)[:, None, :]
    own_grad = at.to_tokens(d_output)

    segments = segment_ids[0]
    base = jnp.stack([(col ^ k) * col_tokens + row * t for k in range(4)]).astype(jnp.int32)
    pos = base[:, None] + jnp.arange(t, dtype=jnp.int32)[None, :]
    seg_rows = jnp.stack([lax.dynamic_slice_in_dim(segments, base[k], t, 0) for k in range(4)])
    low = jnp.sum((segments[None, None, :] < seg_rows[:, :, None]).astype(jnp.int32), axis=2)
    attention = Attention(t, 4, hidden, length, head)
    span = attention.span
    bounds = jnp.stack([low[:, 0] // span, (base + t - 1) // span + 1], axis=1)
    low, pos = low[:, None, :], pos[:, None, :]

    centred_one, inv_one = norm_parts(own)
    normed_one = (centred_one * gain_one + bias_one).astype(bf16)
    block_one = line_second(normed_one, *tie(*line_first(normed_one)))
    block_one, own_grad = tie(block_one, own_grad)
    kv_bias = jnp.pad(b_value.astype(f32), (head, 0))
    kv = (dot_nn(block_one, qkv_weight[:, hidden:]) + kv_bias).astype(bf16)
    got = at.exchange(lambda r: kv)
    queries = (dot_nn(block_one, qkv_weight[:, :hidden]) + b_query.astype(f32)).astype(bf16)
    grad_first = line_first(own_grad)
    kv = at.by_tokens(got, col, t)
    keys, values = kv[:, :head], kv[:, head:]
    attended, lse = attention.forward(bounds, queries, keys, values, low, pos)

    part = dot_nt(attended, out_weight).astype(bf16)
    part, grad_first = tie(part, grad_first)
    block_grad = line_second(own_grad, *grad_first)
    end, near = line_scatter_first(part)
    far = line_scatter_second(part, end)
    near, far, block_grad = tie(near, far, block_grad)
    hidden_one = own + out_bias + line_total(part, near, far)
    centred_two, inv_two = norm_parts(hidden_one)
    normed_two = (centred_two * gain_two + bias_two).astype(bf16)
    far, near = line_first(normed_two)
    grad_act = multiply(block_grad, down_weight, "nt")
    far, near, grad_act = tie(far, near, grad_act)
    block_two = line_second(normed_two, far, near)

    core = at.dp.astype(jnp.int32).reshape(1)
    activated, grad_upper = feed_forward(block_two, up_weight, b_up.astype(f32)[None, :], grad_act)
    part = multiply(grad_upper, up_weight, "nt")
    part, activated, grad_upper = tie(part, activated, grad_upper)
    end, near = line_scatter_first(part)
    down_part = outer(1 - core, activated, block_grad, 0)
    up_part = outer(1 - core, block_two, grad_upper, 1)
    end, down_part, up_part, activated, grad_upper = tie(end, down_part, up_part, activated, grad_upper)
    far = line_scatter_second(part, end)
    down_part, up_part = swap(down_part, "dp"), swap(up_part, "dp")
    down_part = outer(core, activated, block_grad, 0, down_part)
    up_part = outer(core, block_two, grad_upper, 1, up_part)
    near, far, down_part, up_part, activated = tie(near, far, down_part, up_part, activated)
    down_part = scatter_row(down_part, 1)
    up_part = scatter_row(up_part, 0)
    grad_hidden, grad_branch, sums_two = norm_back(
        part, near, far, own_grad, centred_two, inv_two, gain_two
    )
    far, near = line_first(grad_branch)
    far, near, activated = tie(far, near, activated)
    block_branch = line_second(grad_branch, far, near)
    grad_att = dot_nn(block_branch, out_weight).astype(bf16)
    grad_query, grad_kv = attention.backward(
        bounds, queries, attended, grad_att, lse, keys, values, low, pos
    )

    grad_kv = grad_kv.astype(bf16)
    grad_query, grad_kv, block_branch, attended, activated = tie(
        grad_query, grad_kv, block_branch, attended, activated
    )
    final_part = multiply(activated, down_weight, "nn", 1)
    part = dot_nt(grad_query, qkv_weight[:, :hidden]).astype(bf16)
    end, near = line_scatter_first(part)
    kv_grad = at.sum_rows(lambda r: at.line_tokens(grad_kv, col, r, t)).astype(bf16)
    far = line_scatter_second(part, end)
    kv_grad, grad_query, block_one, down_part = tie(kv_grad, grad_query, block_one, down_part)
    parts = [dot_tn(block_one, grad_query).astype(bf16), dot_tn(block_branch, attended).astype(bf16)]
    qo_part = jnp.concatenate(parts, axis=1)
    cut = lambda k: kv_grad[k * t : (k + 1) * t]
    got = swap(jnp.concatenate([cut(1), cut(3)], axis=0), "cl")
    got, final_part, qo_part = tie(got, final_part, qo_part)
    kv_own = add(add(cut(0), got[:t]), swap(add(cut(2), got[t:]), "ch"))
    final_end, final_near = line_scatter_first(final_part)
    near, far, kv_own = tie(near, far, kv_own)
    qo_part = lax.psum_scatter(qo_part, ("ry", "rx", "dp"), scatter_dimension=0, tiled=True)
    unused, grad_own, sums_one = norm_back(
        part, near, far, grad_hidden, centred_one, inv_one, gain_one, kv_own, qkv_weight[:, hidden : hidden + 2 * head]
    )

    kv_part = dot_tn(kv_own, normed_one).astype(bf16)
    kv_far = swap(lax.dynamic_slice_in_dim(kv_part, (1 - at.dp) * head, head, 0), "dp")
    kv_part = add(half_of(kv_part, 0), kv_far)

    sums = lambda a: jnp.sum(a.astype(f32), axis=0)
    tiled = lambda a: jnp.tile(a.reshape(-1, row_width), (1, rows))
    place = lambda a: lax.dynamic_update_slice_in_dim(jnp.zeros((4 * a.shape[0],), f32), a, col * a.shape[0], 0)
    parts = [
        sums_two[:3],
        sums(own_grad)[None],
        tiled(jnp.pad(sums(kv_own[:, head:]), (0, row_width - head))),
        tiled(place(sums(grad_query))),
        tiled(place(sums(grad_upper))),
    ]
    n = sum(p.shape[0] for p in parts)
    parts.append(jnp.zeros((-n % 16, width), f32))
    packed = jnp.concatenate(parts).astype(bf16)
    n = packed.shape[0]
    late = jnp.pad(sums_one, ((0, 8), (0, 0))).astype(bf16)
    grad_own, final_end, down_part, up_part = tie(grad_own, final_end, down_part, up_part)
    final_far = line_scatter_second(final_part, final_end)
    grad_w_down = at.both_cores(down_part, 0)
    got = at.exchange(*(lanes_of(a, row_width) for a in (packed, late, kv_part, grad_own)))
    n = n + 16
    total = sum(g[: n + head].astype(f32) for g in got)
    grad_tokens = at.by_rows(got, n + head, n + head + t).astype(f32)
    total, final_near, final_far = tie(total, final_near, final_far)
    final = hidden_one + down_bias + line_total(final_part, final_near, final_far)
    output = at.by_rows(at.exchange(lanes_of(final.astype(bf16), row_width)), 0, t)
    total = total.astype(bf16)
    both = lax.ppermute(total, ("ch", "cl"), [(0, 3), (3, 0), (1, 2), (2, 1)])
    sides = [total, swap(total, "ch"), swap(total, "cl"), both]
    lower = (sides[0].astype(f32) + sides[1].astype(f32)) + (sides[2].astype(f32) + sides[3].astype(f32))
    total = lower
    total = gather_axis(total.astype(bf16), "dp").astype(f32)
    grad_w_keyval = total[:, n:].reshape(2 * head, row_width).T
    total = total[0, :n] + total[1, :n]
    qo_part = at.both_cores(qo_part, 0)
    grad_w_query, grad_w_out = qo_part[:, :hidden], qo_part[:, hidden:].T
    grad_w_up = at.both_cores(up_part, 1)
    grad_ln2_gain, grad_ln2_bias, grad_b_out, grad_b_down = total[:4]
    grad_ln1_gain, grad_ln1_bias = total[n - 16], total[n - 15]
    grad_b_value = total[4, :head]
    of_col = lambda first, n: lax.dynamic_slice_in_dim(
        total[first : first + 4 * n // row_width].reshape(-1), col * n, n, 0
    )
    grad_b_query = of_col(5, hidden)
    grad_b_up = of_col(5 + 4 * hidden // row_width, b_up.shape[0])
    return (
        output,
        grad_tokens,
        grad_ln1_gain,
        grad_ln1_bias,
        grad_w_query,
        grad_b_query,
        grad_w_keyval,
        grad_b_value,
        grad_w_out,
        grad_b_out,
        grad_ln2_gain,
        grad_ln2_bias,
        grad_w_up,
        grad_b_up,
        grad_w_down,
        grad_b_down,
    )


def solution(mesh):
    dp, rows, cols = (mesh.shape[name] for name in ("dp", "row", "col"))
    fine = Mesh(
        mesh.devices.reshape(dp, rows // 2, 2, cols // 2, 2), ("dp", "ry", "rx", "ch", "cl")
    )
    row, col = ("ry", "rx"), ("ch", "cl")
    tok = P(("dp", "ch", "cl"), row)
    in_specs = (
        tok,
        P("dp", None),
        P(row),
        P(row),
        P(row, col),
        P(col),
        P(row, None),
        P(),
        P(col, row),
        P(row),
        P(row),
        P(row),
        P(row, col),
        P(col),
        P(col, row),
        P(row),
        tok,
    )
    out_specs = (
        tok,
        tok,
        P(row),
        P(row),
        P(row, col),
        P(col),
        P(row, None),
        P(),
        P(col, row),
        P(row),
        P(row),
        P(row),
        P(row, col),
        P(col),
        P(col, row),
        P(row),
    )
    return jax.shard_map(
        per_device, mesh=fine, in_specs=in_specs, out_specs=out_specs, check_vma=False
    )
```
